32 devices in a mesh: seq: 4 (over y, x), chan: 8 (over z, core).
Axes of the slice: x: 2, y: 2, z: 4, core: 2. Of those that a mesh axis runs over, the one named last changes fastest.
Arguments:
- query_stream: bfloat16 [1024, 8192], P('seq', 'chan'), may hold values from -300 to 300
- key_stream: bfloat16 [1024, 8192], P('seq', 'chan'), may hold values from -6 to 6
- value_stream: bfloat16 [1024, 8192], P('seq', 'chan'), may hold values from -6 to 6
- short_filters: float32 [3, 7, 8192], P(None, None, 'chan'), may hold values from -3.5 to 3.5
- long_filter: bfloat16 [1024, 8192], P('seq', 'chan'), may hold values from -0.1875 to 0.1875
- skip_bias: float32 [8192], P('chan'), may hold values from -4 to 4
- norm_gain: float32 [8192], P('chan'), may hold values from 0.5 to 1.5
Outputs:
- normed_output: float32 [1024, 8192], P('seq', 'chan')
The draws below stay inside these ranges and needn't reach their ends.
All inputs are finite; a program needn't handle non-finite values.
Results may differ from the reference program's by a relative error of at most 0.01.
Values may be sent and summed in bfloat16 or wider, within the bound.
A program may use at most 64 MiB of HBM per device.

```python
import math
import jax
import jax.numpy as jnp
from jax import lax

D = 8192
TAPS = 7
TOKENS = 1024


def draw_query_stream(key, part):
    key_rows, key_cols, key_base = jax.random.split(jax.random.fold_in(key, 11), 3)
    row_scale = jnp.exp(jax.random.uniform(key_rows, (TOKENS, 1), jnp.float32) * math.log(10.0))
    ramp = jnp.exp(math.log(3.0) * jnp.arange(D, dtype=jnp.float32) / (D - 1)).reshape(1, D)
    col_scale = ramp * jnp.exp(jax.random.uniform(key_cols, (1, D), jnp.float32) * math.log(3.3))
    base = jnp.clip(jax.random.normal(key_base, (TOKENS, D), jnp.float32), -3.0, 3.0)
    return (base * row_scale * col_scale).astype(jnp.bfloat16)


def levels(own_key, extent, cuts, least, high):
    factor_of = 1.0
    for axis_at, blocks in cuts:
        steps = jax.random.uniform(jax.random.fold_in(jax.random.fold_in(own_key, 6), axis_at), (blocks,), jnp.float32, least / len(cuts), high / len(cuts))
        factor_of = factor_of * jnp.repeat(jnp.exp(steps), extent[axis_at] // blocks).reshape((-1,) + (1,) * (len(extent) - 1 - axis_at))
    return factor_of


def noise(rng, dims, scale, most, cuts=(), kind=jnp.bfloat16):
    level = levels(rng, dims, cuts, -0.22, 0.18) if cuts else 1.0
    drawn = jax.random.normal(rng, dims, jnp.float32) * scale * level
    return jnp.minimum(jnp.maximum(drawn, -most), most).astype(kind)


def setup_inputs(seed: int = 0) -> dict:
    splits = jax.random.split(jax.random.key(seed), 8)
    return {
        "query_stream": draw_query_stream(jax.random.fold_in(splits[7], 71), 0),
        "key_stream": noise(splits[1], (TOKENS, D), 1.0, 6.0, ((0, 4), (1, 8))),
        "value_stream": noise(splits[2], (TOKENS, D), 1.0, 6.0, ((0, 4), (1, 8))),
        "short_filters": noise(splits[3], (3, TAPS, D), 3 ** -0.5, 3.5, ((2, 8),), jnp.float32),
        "long_filter": noise(splits[4], (TOKENS, D), TOKENS ** -0.5, 0.1875, ((0, 4), (1, 8))),
        "skip_bias": noise(splits[5], (D,), 1.0, 4.0, ((0, 8),), jnp.float32),
        "norm_gain": jnp.clip(1.0 + 0.1 * jax.random.normal(splits[6], (D,), jnp.float32), 0.5, 1.5),
    }


def short_conv(stream, weights):
    length = stream.shape[0]
    padded = jnp.pad(stream, ((TAPS - 1, 0), (0, 0)))
    result = jnp.zeros_like(stream)
    for offset in range(TAPS):
        start = TAPS - 1 - offset
        result = result + weights[offset][None, :] * padded[start:start + length]
    return result

def channel_block(inputs):
    query_part, key_part, value_part, filters_part, long_part, bias_part = inputs
    query_conv = short_conv(query_part.astype(jnp.float32), filters_part[0])
    key_conv = short_conv(key_part.astype(jnp.float32), filters_part[1])
    value_conv = short_conv(value_part.astype(jnp.float32), filters_part[2])
    gated = (key_conv * value_conv).astype(jnp.bfloat16).astype(jnp.float32)
    length = gated.shape[0]
    spectrum = jnp.fft.rfft(gated, n=2 * length, axis=0) * jnp.fft.rfft(long_part.astype(jnp.float32), n=2 * length, axis=0)
    long_out = jnp.fft.irfft(spectrum, n=2 * length, axis=0)[:length]
    return jax.nn.silu(query_conv * (long_out + bias_part[None, :] * gated))

def reference(query_stream, key_stream, value_stream, short_filters, long_filter, skip_bias, norm_gain):
    block_width = math.gcd(D, 512)
    blocks = D // block_width

    def split(array):
        return array.reshape(TOKENS, blocks, block_width).transpose(1, 0, 2)
    filters_split = short_filters.reshape(3, TAPS, blocks, block_width).transpose(2, 0, 1, 3)
    bias_split = skip_bias.reshape(blocks, block_width)
    mixed_blocks = lax.map(channel_block, (split(query_stream), split(key_stream), split(value_stream), filters_split, split(long_filter), bias_split))
    mixed = mixed_blocks.transpose(1, 0, 2).reshape(TOKENS, D)
    row_power = lax.optimization_barrier(jnp.sum(mixed * mixed, axis=1))
    return mixed * lax.rsqrt(row_power / D + 1e-06)[:, None] * norm_gain[None, :]
```

```python
import functools
import math

import jax
import jax.numpy as jnp
import numpy as np
from jax import lax
from jax.experimental import pallas as pl
from jax.experimental.pallas import tpu as pltpu
from jax.sharding import PartitionSpec as P

D = 8192


def from_behind(value, axis, steps):
    count = lax.axis_size(axis)
    first, last = (max(0, -steps), min(count, count - steps))
    return lax.ppermute(value, axis, [(source, source + steps) for source in range(first, last)])


def rotation(first_index, second_index, period):
    product = first_index[:, None] * second_index[None, :] % period
    angle = product.astype(jnp.float32) * (2.0 * math.pi / period)
    return (jnp.cos(angle), jnp.sin(angle))


def halves(values):
    upper = values.astype(jnp.bfloat16)
    lower = (values - upper.astype(jnp.float32)).astype(jnp.bfloat16)
    return (upper, lower)


def mixing(table, operand, form):
    table_high, table_low = halves(table)
    if operand.dtype == jnp.bfloat16:
        pairs = [(table_high, operand), (table_low, operand)]
    else:
        operand_high, operand_low = halves(operand)
        pairs = [(table_high, operand_high), (table_low, operand_high), (table_high, operand_low)]
    total = None
    for left, right in pairs:
        term = jnp.einsum(form, left, right, preferred_element_type=jnp.float32)
        total = term if total is None else total + term
    return total


def swapped_convolution(gated, long_filter):
    block_rows, local_width = gated.shape
    seq_count = lax.axis_size("seq")
    full_length = 2 * seq_count * block_rows
    signal_in, filter_in = (
        lax.all_to_all(gated[:, None, :], "seq", split_axis=2, concat_axis=1, tiled=True),
        lax.all_to_all(long_filter[:, None, :], "seq", split_axis=2, concat_axis=1, tiled=True),
    )
    freq_short = jnp.arange(2 * seq_count, dtype=jnp.int32)
    cos_short, sin_short = rotation(
        freq_short, jnp.arange(seq_count, dtype=jnp.int32), 2 * seq_count
    )
    long_index = jnp.arange(block_rows, dtype=jnp.int32)
    cos_turn, sin_turn = rotation(long_index, freq_short, full_length)
    cos_turn = cos_turn[:, :, None]
    sin_turn = sin_turn[:, :, None]
    cos_long, sin_long = rotation(long_index, long_index, block_rows)

    def transform(signal):
        real_part = mixing(cos_short, signal, "km,jmc->jkc")
        imag_part = -mixing(sin_short, signal, "km,jmc->jkc")
        twisted_real = (real_part * cos_turn + imag_part * sin_turn).reshape(block_rows, -1)
        twisted_imag = (imag_part * cos_turn - real_part * sin_turn).reshape(block_rows, -1)
        out_real = mixing(cos_long, twisted_real, "kj,jc->kc") + mixing(
            sin_long, twisted_imag, "kj,jc->kc"
        )
        out_imag = mixing(cos_long, twisted_imag, "kj,jc->kc") - mixing(
            sin_long, twisted_real, "kj,jc->kc"
        )
        return (out_real, out_imag)

    signal_real, signal_imag = transform(signal_in)
    filter_real, filter_imag = transform(filter_in)
    prod_real = signal_real * filter_real - signal_imag * filter_imag
    prod_imag = signal_real * filter_imag + signal_imag * filter_real
    back_real = mixing(cos_long, prod_real, "kj,jc->kc") - mixing(sin_long, prod_imag, "kj,jc->kc")
    back_imag = mixing(sin_long, prod_real, "kj,jc->kc") + mixing(cos_long, prod_imag, "kj,jc->kc")
    back_real = back_real.reshape(block_rows, 2 * seq_count, -1)
    back_imag = back_imag.reshape(block_rows, 2 * seq_count, -1)
    turned_real = back_real * cos_turn - back_imag * sin_turn
    turned_imag = back_real * sin_turn + back_imag * cos_turn
    result = (
        mixing(cos_short.T, turned_real, "mk,jkc->jmc")
        - mixing(sin_short.T, turned_imag, "mk,jkc->jmc")
    ) / full_length
    gathered = lax.all_to_all(result, "seq", split_axis=1, concat_axis=2, tiled=True)
    return gathered.reshape(block_rows, local_width)


def shards(
    query_stream, key_stream, value_stream, short_filters, long_filter, skip_bias, norm_gain
):
    block_rows = query_stream.shape[0]
    tap_count = short_filters.shape[1]
    stacked = jnp.stack([query_stream, key_stream, value_stream])
    previous = from_behind(stacked[:, block_rows - tap_count + 1 :, :], "seq", 1)
    extended = jnp.concatenate([previous, stacked], axis=1).astype(jnp.float32)
    convolved = jnp.zeros(stacked.shape, jnp.float32)
    for offset in range(tap_count):
        start = tap_count - 1 - offset
        convolved = (
            convolved
            + short_filters[:, offset, None, :] * extended[:, start : start + block_rows, :]
        )
    query_conv = convolved[0]
    gated = (convolved[1] * convolved[2]).astype(jnp.bfloat16)
    long_out = swapped_convolution(gated, long_filter)
    mixed = jax.nn.silu(query_conv * (long_out + skip_bias[None, :] * gated.astype(jnp.float32)))
    row_power = lax.psum(jnp.sum(mixed * mixed, axis=1), "chan")
    return mixed * lax.rsqrt(row_power / D + 1e-06)[:, None] * norm_gain[None, :]


MESH = pl.DeviceIdType.MESH
PACK = 16
LANES = 128
VMEM_BYTES = 60 * 1024 * 1024


def tables(tokens, parts):
    freq = 2 * np.arange(tokens, dtype=np.int64) + 1
    time = np.arange(tokens, dtype=np.int64)
    angle = (freq[:, None] * time[None, :] % (4 * tokens)) * (2.0 * np.pi / (4 * tokens))
    forward = np.concatenate([np.cos(angle), -np.sin(angle)], axis=0)
    backward = forward.T / tokens
    rows = tokens // parts
    forward = forward.reshape(2 * tokens, parts, rows).transpose(1, 0, 2)
    backward = backward.reshape(parts, rows, 2 * tokens)
    return (forward.astype(jnp.bfloat16), backward.astype(jnp.bfloat16))


def kernel(
    parts,
    groups,
    query,
    key,
    value,
    taps_in,
    filt,
    skip_in,
    forward_in,
    backward_in,
    mixed_out,
    power_out,
    extended,
    taps,
    skip,
    forward,
    backward,
    filter_all,
    gated,
    gated_all,
    query_conv,
    spectrum,
    filter_spectrum,
    product,
    result,
    result_all,
    mixed,
    partial,
    power,
    power_all,
    load_sem,
    halo_send,
    halo_recv,
    filter_send,
    filter_recv,
    gated_send,
    gated_recv,
    result_send,
    result_recv,
    power_send,
    power_recv,
    store_sem,
):
    me = lax.axis_index("seq")
    group = lax.axis_index("chan")
    rows, width = gated.shape
    part = width // parts
    tokens = rows * parts
    tap_count = taps.shape[1]

    def columns(owner):
        return pl.ds(pl.multiple_of(owner * part, LANES), part)

    def peer(distance):
        return lax.rem(me + distance, parts)

    def source(distance):
        return lax.rem(me + parts - distance, parts)

    streams = (key, value, query)
    loads = []
    for index, (src, dst) in enumerate(
        (
            (key, extended.at[0, pl.ds(PACK, rows), :]),
            (value, extended.at[1, pl.ds(PACK, rows), :]),
            (taps_in, taps),
            (query, extended.at[2, pl.ds(PACK, rows), :]),
            (filt.at[:, columns(me)], filter_all.at[me]),
            (forward_in, forward),
            (skip_in, skip),
            (backward_in, backward),
        )
    ):
        copy = pltpu.make_async_copy(src, dst, load_sem.at[index])
        copy.start()
        loads.append(copy)

    barrier = pltpu.get_barrier_semaphore()
    for distance in range(1, parts):
        pl.semaphore_signal(
            barrier, inc=1, device_id={"seq": peer(distance)}, device_id_type=MESH
        )
    for distance in range(1, groups):
        pl.semaphore_signal(
            barrier,
            inc=1,
            device_id={"chan": lax.rem(group + distance, groups)},
            device_id_type=MESH,
        )
    pl.semaphore_wait(barrier, parts + groups - 2)

    halos = []
    for index in range(3):
        copy = pltpu.make_async_remote_copy(
            src_ref=streams[index].at[pl.ds(rows - PACK, PACK), :],
            dst_ref=extended.at[index, pl.ds(0, PACK), :],
            send_sem=halo_send.at[index],
            recv_sem=halo_recv.at[index],
            device_id={"seq": peer(1)},
            device_id_type=MESH,
        )
        copy.start()
        halos.append(copy)

    def exchange(src, dst, send_sem, recv_sem, distance):
        copy = pltpu.make_async_remote_copy(
            src_ref=src,
            dst_ref=dst.at[me],
            send_sem=send_sem.at[distance - 1],
            recv_sem=recv_sem.at[distance - 1],
            device_id={"seq": peer(distance)},
            device_id_type=MESH,
        )
        copy.start()
        return copy

    filter_copies = [
        exchange(filt.at[:, columns(peer(d))], filter_all, filter_send, filter_recv, d)
        for d in range(1, parts)
    ]

    def ready(index):
        halos[index].wait_recv()

        @pl.when(me == 0)
        def _():
            extended[index, pl.ds(0, PACK), :] = jnp.zeros((PACK, width), extended.dtype)

    block = 64
    tiles = part // LANES

    def short(index, weight, start, lanes):
        window = extended[index, pl.ds(start, block + PACK), lanes].astype(jnp.float32)
        total = taps[weight, pl.ds(0, 1), lanes] * window[PACK:]
        for tap in range(1, tap_count):
            total = total + taps[weight, pl.ds(tap, 1), lanes] * pltpu.roll(window, tap, 0)[PACK:]
        return total

    for index in range(3):
        loads[index].wait()
    ready(0)
    ready(1)

    gated_copies = []
    for d in (*range(1, parts), 0):
        owner = peer(d)

        def gate(step, _, owner=owner):
            start = pl.multiple_of(step // tiles * block, block)
            lanes = pl.ds(pl.multiple_of(owner * part + step % tiles * LANES, LANES), LANES)
            gated[pl.ds(start, block), lanes] = (
                short(0, 1, start, lanes) * short(1, 2, start, lanes)
            ).astype(gated.dtype)
            return 0

        lax.fori_loop(0, rows // block * tiles, gate, 0)
        if d:
            gated_copies.append(
                exchange(gated.at[:, columns(owner)], gated_all, gated_send, gated_recv, d)
            )

    loads[3].wait()
    ready(2)

    def query_step(step, _):
        start = pl.multiple_of(step // (width // LANES) * block, block)
        lanes = pl.ds(pl.multiple_of(step % (width // LANES) * LANES, LANES), LANES)
        query_conv[pl.ds(start, block), lanes] = short(2, 0, start, lanes)
        return 0

    lax.fori_loop(0, rows // block * (width // LANES), query_step, 0)

    loads[4].wait()
    loads[5].wait()
    for copy in filter_copies:
        copy.wait_recv()
    tile = 256

    def filter_step(step, _):
        at = pl.ds(pl.multiple_of(step * tile, tile), tile)
        total = None
        for j in range(parts):
            term = jnp.dot(
                forward[j, at, :], filter_all[j], preferred_element_type=jnp.float32
            )
            total = term if total is None else total + term
        filter_spectrum[at, :] = total
        return 0

    lax.fori_loop(0, 2 * tokens // tile, filter_step, 0)

    wide = 512

    def accumulate(owner, operand, first):
        def step_body(step, _):
            at = pl.ds(pl.multiple_of(step * wide, wide), wide)
            term = jnp.dot(forward[owner, at, :], operand(), preferred_element_type=jnp.float32)
            spectrum[at, :] = term if first else spectrum[at, :] + term
            return 0

        lax.fori_loop(0, 2 * tokens // wide, step_body, 0)

    accumulate(me, lambda: gated[:, columns(me)], True)
    for d in range(1, parts):
        gated_copies[d - 1].wait_recv()
        owner = source(d)
        accumulate(owner, lambda: gated_all[owner], False)

    def product_step(step, _):
        real = pl.ds(pl.multiple_of(step * 64, 64), 64)
        imag = pl.ds(pl.multiple_of(tokens + step * 64, 64), 64)
        a, b = spectrum[real, :], spectrum[imag, :]
        c, d = filter_spectrum[real, :], filter_spectrum[imag, :]
        product[real, :] = (a * c - b * d).astype(product.dtype)
        product[imag, :] = (a * d + b * c).astype(product.dtype)
        return 0

    lax.fori_loop(0, tokens // 64, product_step, 0)

    loads[7].wait()
    result_copies = []
    for d in (*range(1, parts), 0):
        owner = peer(d)
        result[owner] = jnp.dot(
            backward[owner], product[...], preferred_element_type=jnp.float32
        ).astype(result.dtype)
        if d:
            result_copies.append(
                exchange(result.at[owner], result_all, result_send, result_recv, d)
            )

    loads[6].wait()
    partial[...] = jnp.zeros_like(partial)
    stores = []

    def finish(owner, fetch, index):
        def step_body(step, _):
            start = pl.multiple_of(step // tiles * block, block)
            inner = step % tiles * LANES
            lanes = pl.ds(pl.multiple_of(owner * part + inner, LANES), LANES)
            at = pl.ds(start, block)
            long_out = fetch(at, pl.ds(pl.multiple_of(inner, LANES), LANES)).astype(jnp.float32)
            direct = skip[:, lanes] * gated[at, lanes].astype(jnp.float32)
            x = query_conv[at, lanes] * (long_out + direct)
            y = x / (1.0 + jnp.exp(-x))
            mixed[at, lanes] = y
            partial[at, :] = partial[at, :] + y * y
            return 0

        lax.fori_loop(0, rows // block * tiles, step_body, 0)
        copy = pltpu.make_async_copy(
            mixed.at[:, columns(owner)], mixed_out.at[:, columns(owner)], store_sem.at[index]
        )
        copy.start()
        stores.append(copy)

    finish(me, lambda at, lanes: result[me, at, lanes], 0)
    for d in range(1, parts):
        result_copies[d - 1].wait_recv()
        owner = source(d)
        finish(owner, lambda at, lanes: result_all[owner, at, lanes], d)

    power[...] = jnp.broadcast_to(
        jnp.sum(partial[...].T, axis=0, keepdims=True), power.shape
    )
    power_copies = []
    for distance in range(1, groups):
        copy = pltpu.make_async_remote_copy(
            src_ref=power,
            dst_ref=power_all.at[group],
            send_sem=power_send.at[distance - 1],
            recv_sem=power_recv.at[distance - 1],
            device_id={"chan": lax.rem(group + distance, groups)},
            device_id_type=MESH,
        )
        copy.start()
        power_copies.append(copy)
    power_all[group] = power[...]
    for copy in (*halos, *filter_copies, *gated_copies, *result_copies):
        copy.wait_send()
    for copy in power_copies:
        copy.wait()
    power_out[...] = jnp.sum(power_all[...], axis=0)
    for copy in stores:
        copy.wait()


def fused(
    query_stream, key_stream, value_stream, short_filters, long_filter, skip_bias, norm_gain
):
    rows, width = query_stream.shape
    parts = lax.axis_size("seq")
    groups = lax.axis_size("chan")
    tokens = rows * parts
    part = width // parts
    forward, backward = tables(tokens, parts)
    dma = pltpu.SemaphoreType.DMA
    bf16, f32 = jnp.bfloat16, jnp.float32
    mixed, power = pl.pallas_call(
        functools.partial(kernel, parts, groups),
        out_shape=(
            jax.ShapeDtypeStruct((rows, width), f32),
            jax.ShapeDtypeStruct((8, rows), f32),
        ),
        in_specs=[pl.BlockSpec(memory_space=pl.ANY)] * 8,
        out_specs=(
            pl.BlockSpec(memory_space=pl.ANY),
            pl.BlockSpec(memory_space=pltpu.VMEM),
        ),
        scratch_shapes=[
            pltpu.VMEM((3, rows + PACK, width), bf16),
            pltpu.VMEM(short_filters.shape, f32),
            pltpu.VMEM((1, width), f32),
            pltpu.VMEM(forward.shape, bf16),
            pltpu.VMEM(backward.shape, bf16),
            pltpu.VMEM((parts, rows, part), bf16),
            pltpu.VMEM((rows, width), bf16),
            pltpu.VMEM((parts, rows, part), bf16),
            pltpu.VMEM((rows, width), f32),
            pltpu.VMEM((2 * tokens, part), f32),
            pltpu.VMEM((2 * tokens, part), f32),
            pltpu.VMEM((2 * tokens, part), bf16),
            pltpu.VMEM((parts, rows, part), bf16),
            pltpu.VMEM((parts, rows, part), bf16),
            pltpu.VMEM((rows, width), f32),
            pltpu.VMEM((rows, LANES), f32),
            pltpu.VMEM((8, rows), f32),
            pltpu.VMEM((groups, 8, rows), f32),
            dma((8,)),
            dma((3,)),
            dma((3,)),
            dma((parts - 1,)),
            dma((parts - 1,)),
            dma((parts - 1,)),
            dma((parts - 1,)),
            dma((parts - 1,)),
            dma((parts - 1,)),
            dma((groups - 1,)),
            dma((groups - 1,)),
            dma((parts,)),
        ],
        compiler_params=pltpu.CompilerParams(
            collective_id=0, has_side_effects=True, vmem_limit_bytes=VMEM_BYTES
        ),
    )(
        query_stream,
        key_stream,
        value_stream,
        short_filters,
        long_filter,
        skip_bias[None, :],
        jnp.asarray(forward),
        jnp.asarray(backward),
    )
    scale = lax.rsqrt(power[0] / (width * groups) + 1e-06)
    return mixed * scale[:, None] * norm_gain[None, :]


def dense_fits(mesh, shape):
    tokens, channels = shape
    part = channels // (mesh.shape["chan"] * mesh.shape["seq"])
    rows = tokens // mesh.shape["seq"]
    return (
        part % LANES == 0
        and rows % 256 == 0
        and mesh.shape["seq"] > 1
        and mesh.shape["chan"] > 1
        and 8 * tokens * tokens <= VMEM_BYTES // 4
    )


def solution(mesh):
    placed = (
        P("seq", "chan"),
        P("seq", "chan"),
        P("seq", "chan"),
        P(None, None, "chan"),
        P("seq", "chan"),
        P("chan"),
        P("chan"),
    )

    def apply(query_stream, *others):
        body = fused if dense_fits(mesh, query_stream.shape) else shards
        return jax.shard_map(
            body, mesh=mesh, in_specs=placed, out_specs=P("seq", "chan"), check_vma=False
        )(query_stream, *others)

    return apply
```

```python
import functools
import math

import jax
import jax.numpy as jnp
import numpy as np
from jax import lax
from jax.experimental import pallas as pl
from jax.experimental.pallas import tpu as pltpu
from jax.sharding import PartitionSpec as P

D = 8192


def from_behind(value, axis, steps):
    count = lax.axis_size(axis)
    first, last = (max(0, -steps), min(count, count - steps))
    return lax.ppermute(value, axis, [(source, source + steps) for source in range(first, last)])


def rotation(first_index, second_index, period):
    product = first_index[:, None] * second_index[None, :] % period
    angle = product.astype(jnp.float32) * (2.0 * math.pi / period)
    return (jnp.cos(angle), jnp.sin(angle))


def halves(values):
    upper = values.astype(jnp.bfloat16)
    lower = (values - upper.astype(jnp.float32)).astype(jnp.bfloat16)
    return (upper, lower)


def mixing(table, operand, form):
    table_high, table_low = halves(table)
    if operand.dtype == jnp.bfloat16:
        pairs = [(table_high, operand), (table_low, operand)]
    else:
        operand_high, operand_low = halves(operand)
        pairs = [(table_high, operand_high), (table_low, operand_high), (table_high, operand_low)]
    total = None
    for left, right in pairs:
        term = jnp.einsum(form, left, right, preferred_element_type=jnp.float32)
        total = term if total is None else total + term
    return total


def swapped_convolution(gated, long_filter):
    block_rows, local_width = gated.shape
    seq_count = lax.axis_size("seq")
    full_length = 2 * seq_count * block_rows
    signal_in, filter_in = (
        lax.all_to_all(gated[:, None, :], "seq", split_axis=2, concat_axis=1, tiled=True),
        lax.all_to_all(long_filter[:, None, :], "seq", split_axis=2, concat_axis=1, tiled=True),
    )
    freq_short = jnp.arange(2 * seq_count, dtype=jnp.int32)
    cos_short, sin_short = rotation(
        freq_short, jnp.arange(seq_count, dtype=jnp.int32), 2 * seq_count
    )
    long_index = jnp.arange(block_rows, dtype=jnp.int32)
    cos_turn, sin_turn = rotation(long_index, freq_short, full_length)
    cos_turn = cos_turn[:, :, None]
    sin_turn = sin_turn[:, :, None]
    cos_long, sin_long = rotation(long_index, long_index, block_rows)

    def transform(signal):
        real_part = mixing(cos_short, signal, "km,jmc->jkc")
        imag_part = -mixing(sin_short, signal, "km,jmc->jkc")
        twisted_real = (real_part * cos_turn + imag_part * sin_turn).reshape(block_rows, -1)
        twisted_imag = (imag_part * cos_turn - real_part * sin_turn).reshape(block_rows, -1)
        out_real = mixing(cos_long, twisted_real, "kj,jc->kc") + mixing(
            sin_long, twisted_imag, "kj,jc->kc"
        )
        out_imag = mixing(cos_long, twisted_imag, "kj,jc->kc") - mixing(
            sin_long, twisted_real, "kj,jc->kc"
        )
        return (out_real, out_imag)

    signal_real, signal_imag = transform(signal_in)
    filter_real, filter_imag = transform(filter_in)
    prod_real = signal_real * filter_real - signal_imag * filter_imag
    prod_imag = signal_real * filter_imag + signal_imag * filter_real
    back_real = mixing(cos_long, prod_real, "kj,jc->kc") - mixing(sin_long, prod_imag, "kj,jc->kc")
    back_imag = mixing(sin_long, prod_real, "kj,jc->kc") + mixing(cos_long, prod_imag, "kj,jc->kc")
    back_real = back_real.reshape(block_rows, 2 * seq_count, -1)
    back_imag = back_imag.reshape(block_rows, 2 * seq_count, -1)
    turned_real = back_real * cos_turn - back_imag * sin_turn
    turned_imag = back_real * sin_turn + back_imag * cos_turn
    result = (
        mixing(cos_short.T, turned_real, "mk,jkc->jmc")
        - mixing(sin_short.T, turned_imag, "mk,jkc->jmc")
    ) / full_length
    gathered = lax.all_to_all(result, "seq", split_axis=1, concat_axis=2, tiled=True)
    return gathered.reshape(block_rows, local_width)


def shards(
    query_stream, key_stream, value_stream, short_filters, long_filter, skip_bias, norm_gain
):
    block_rows = query_stream.shape[0]
    tap_count = short_filters.shape[1]
    stacked = jnp.stack([query_stream, key_stream, value_stream])
    previous = from_behind(stacked[:, block_rows - tap_count + 1 :, :], "seq", 1)
    extended = jnp.concatenate([previous, stacked], axis=1).astype(jnp.float32)
    convolved = jnp.zeros(stacked.shape, jnp.float32)
    for offset in range(tap_count):
        start = tap_count - 1 - offset
        convolved = (
            convolved
            + short_filters[:, offset, None, :] * extended[:, start : start + block_rows, :]
        )
    query_conv = convolved[0]
    gated = (convolved[1] * convolved[2]).astype(jnp.bfloat16)
    long_out = swapped_convolution(gated, long_filter)
    mixed = jax.nn.silu(query_conv * (long_out + skip_bias[None, :] * gated.astype(jnp.float32)))
    row_power = lax.psum(jnp.sum(mixed * mixed, axis=1), "chan")
    return mixed * lax.rsqrt(row_power / D + 1e-06)[:, None] * norm_gain[None, :]


MESH = pl.DeviceIdType.MESH
PACK = 16
LANES = 128
VMEM_BYTES = 60 * 1024 * 1024


def tables(tokens, parts):
    freq = 2 * np.arange(tokens, dtype=np.int64) + 1
    time = np.arange(tokens, dtype=np.int64)
    angle = (freq[:, None] * time[None, :] % (4 * tokens)) * (2.0 * np.pi / (4 * tokens))
    forward = np.concatenate([np.cos(angle), -np.sin(angle)], axis=0)
    backward = forward.T / tokens
    rows = tokens // parts
    forward = forward.reshape(2 * tokens, parts, rows).transpose(1, 0, 2)
    backward = backward.reshape(parts, rows, 2 * tokens)
    return (forward.astype(jnp.bfloat16), backward.astype(jnp.bfloat16))


def kernel(
    parts,
    groups,
    query,
    key,
    value,
    taps_in,
    filt,
    skip_in,
    forward_in,
    backward_in,
    mixed_out,
    power_out,
    extended,
    taps,
    skip,
    forward,
    backward,
    filter_stage,
    filter_all,
    gated,
    gated_all,
    query_conv,
    spectrum,
    filter_spectrum,
    product,
    result,
    result_all,
    mixed,
    partial,
    power,
    power_all,
    load_sem,
    stage_sem,
    halo_send,
    halo_recv,
    filter_send,
    filter_recv,
    gated_send,
    gated_recv,
    result_send,
    result_recv,
    power_send,
    power_recv,
    store_sem,
):
    me = lax.axis_index("seq")
    group = lax.axis_index("chan")
    rows, width = mixed.shape
    part = width // parts
    tokens = rows * parts
    tap_count = taps.shape[1]

    def columns(owner):
        return pl.ds(pl.multiple_of(owner * part, LANES), part)

    def peer(distance):
        return lax.rem(me + distance, parts)

    def source(distance):
        return lax.rem(me + parts - distance, parts)

    streams = (key, value, query)
    loads = []
    for index, (src, dst) in enumerate(
        (
            (key, extended.at[0, pl.ds(PACK, rows), :]),
            (value, extended.at[1, pl.ds(PACK, rows), :]),
            (taps_in, taps),
            (query, extended.at[2, pl.ds(PACK, rows), :]),
            (filt.at[:, columns(me)], filter_all.at[me]),
            (forward_in, forward),
            (skip_in, skip),
            (backward_in, backward),
        )
    ):
        loads.append(pltpu.make_async_copy(src, dst, load_sem.at[index]))
    staged = [
        pltpu.make_async_copy(
            filt.at[:, columns(peer(d))], filter_stage.at[peer(d)], stage_sem.at[d - 1]
        )
        for d in range(1, parts)
    ]
    for copy in (*staged, *loads[:5]):
        copy.start()

    barrier = pltpu.get_barrier_semaphore()
    for distance in range(1, parts):
        pl.semaphore_signal(
            barrier, inc=1, device_id={"seq": peer(distance)}, device_id_type=MESH
        )
    for distance in range(1, groups):
        pl.semaphore_signal(
            barrier,
            inc=1,
            device_id={"chan": lax.rem(group + distance, groups)},
            device_id_type=MESH,
        )
    pl.semaphore_wait(barrier, parts + groups - 2)

    halos = []
    for index in range(3):
        copy = pltpu.make_async_remote_copy(
            src_ref=streams[index].at[pl.ds(rows - PACK, PACK), :],
            dst_ref=extended.at[index, pl.ds(0, PACK), :],
            send_sem=halo_send.at[index],
            recv_sem=halo_recv.at[index],
            device_id={"seq": peer(1)},
            device_id_type=MESH,
        )
        copy.start()
        halos.append(copy)

    def exchange(src, dst, send_sem, recv_sem, distance):
        copy = pltpu.make_async_remote_copy(
            src_ref=src,
            dst_ref=dst.at[me],
            send_sem=send_sem.at[distance - 1],
            recv_sem=recv_sem.at[distance - 1],
            device_id={"seq": peer(distance)},
            device_id_type=MESH,
        )
        copy.start()
        return copy

    filter_copies = []
    for d in range(1, parts):
        staged[d - 1].wait()
        filter_copies.append(
            exchange(filter_stage.at[peer(d)], filter_all, filter_send, filter_recv, d)
        )
    for copy in loads[5:]:
        copy.start()

    def ready(index):
        halos[index].wait_recv()

        @pl.when(me == 0)
        def _():
            extended[index, pl.ds(0, PACK), :] = jnp.zeros((PACK, width), extended.dtype)

    block = 64
    tiles = part // LANES

    def short(index, weight, start, lanes):
        window = extended[index, pl.ds(start, block + PACK), lanes].astype(jnp.float32)
        total = taps[weight, pl.ds(0, 1), lanes] * window[PACK:]
        for tap in range(1, tap_count):
            total = total + taps[weight, pl.ds(tap, 1), lanes] * pltpu.roll(window, tap, 0)[PACK:]
        return total

    for index in range(3):
        loads[index].wait()
    ready(0)
    ready(1)

    gated_copies = []
    for d in (*range(1, parts), 0):
        owner = peer(d)

        def gate(step, _, owner=owner):
            start = pl.multiple_of(step // tiles * block, block)
            inner = step % tiles * LANES
            lanes = pl.ds(pl.multiple_of(owner * part + inner, LANES), LANES)
            own_lanes = pl.ds(pl.multiple_of(inner, LANES), LANES)
            gated[owner, pl.ds(start, block), own_lanes] = (
                short(0, 1, start, lanes) * short(1, 2, start, lanes)
            ).astype(gated.dtype)
            return 0

        lax.fori_loop(0, rows // block * tiles, gate, 0)
        if d:
            gated_copies.append(
                exchange(gated.at[owner], gated_all, gated_send, gated_recv, d)
            )

    loads[3].wait()
    ready(2)

    def query_step(step, _):
        start = pl.multiple_of(step // (width // LANES) * block, block)
        lanes = pl.ds(pl.multiple_of(step % (width // LANES) * LANES, LANES), LANES)
        query_conv[pl.ds(start, block), lanes] = short(2, 0, start, lanes)
        return 0

    lax.fori_loop(0, rows // block * (width // LANES), query_step, 0)

    loads[4].wait()
    loads[5].wait()
    for copy in filter_copies:
        copy.wait_recv()
    tile = 256

    def filter_step(step, _):
        at = pl.ds(pl.multiple_of(step * tile, tile), tile)
        total = None
        for j in range(parts):
            term = jnp.dot(
                forward[j, at, :], filter_all[j], preferred_element_type=jnp.float32
            )
            total = term if total is None else total + term
        filter_spectrum[at, :] = total
        return 0

    lax.fori_loop(0, 2 * tokens // tile, filter_step, 0)

    wide = 512

    def accumulate(blocks, first):
        def step_body(step, _):
            at = pl.ds(pl.multiple_of(step * wide, wide), wide)
            total = None if first else spectrum[at, :]
            for owner, held in blocks:
                term = jnp.dot(
                    forward[owner, at, :], held[owner], preferred_element_type=jnp.float32
                )
                total = term if total is None else total + term
            spectrum[at, :] = total
            return 0

        lax.fori_loop(0, 2 * tokens // wide, step_body, 0)

    accumulate(((me, gated),), True)
    for copy in gated_copies:
        copy.wait_recv()
    accumulate([(source(d), gated_all) for d in range(1, parts)], False)

    def product_step(step, _):
        real = pl.ds(pl.multiple_of(step * 64, 64), 64)
        imag = pl.ds(pl.multiple_of(tokens + step * 64, 64), 64)
        a, b = spectrum[real, :], spectrum[imag, :]
        c, d = filter_spectrum[real, :], filter_spectrum[imag, :]
        product[real, :] = (a * c - b * d).astype(product.dtype)
        product[imag, :] = (a * d + b * c).astype(product.dtype)
        return 0

    lax.fori_loop(0, tokens // 64, product_step, 0)

    loads[7].wait()
    result_copies = []
    for d in (*range(1, parts), 0):
        owner = peer(d)
        result[owner] = jnp.dot(
            backward[owner], product[...], preferred_element_type=jnp.float32
        ).astype(result.dtype)
        if d:
            result_copies.append(
                exchange(result.at[owner], result_all, result_send, result_recv, d)
            )

    loads[6].wait()
    partial[...] = jnp.zeros_like(partial)
    stores = []

    def finish(owner, fetch, index):
        def step_body(step, _):
            start = pl.multiple_of(step // tiles * block, block)
            inner = step % tiles * LANES
            lanes = pl.ds(pl.multiple_of(owner * part + inner, LANES), LANES)
            own_lanes = pl.ds(pl.multiple_of(inner, LANES), LANES)
            at = pl.ds(start, block)
            long_out = fetch(at, own_lanes).astype(jnp.float32)
            direct = skip[:, lanes] * gated[owner, at, own_lanes].astype(jnp.float32)
            x = query_conv[at, lanes] * (long_out + direct)
            y = x / (1.0 + jnp.exp(-x))
            mixed[at, lanes] = y
            partial[at, :] = partial[at, :] + y * y
            return 0

        lax.fori_loop(0, rows // block * tiles, step_body, 0)
        copy = pltpu.make_async_copy(
            mixed.at[:, columns(owner)], mixed_out.at[:, columns(owner)], store_sem.at[index]
        )
        copy.start()
        stores.append(copy)

    finish(me, lambda at, lanes: result[me, at, lanes], 0)
    for d in range(1, parts):
        result_copies[d - 1].wait_recv()
        owner = source(d)
        finish(owner, lambda at, lanes: result_all[owner, at, lanes], d)

    power[...] = jnp.broadcast_to(
        jnp.sum(partial[...].T, axis=0, keepdims=True), power.shape
    )
    power_copies = []
    for distance in range(1, groups):
        copy = pltpu.make_async_remote_copy(
            src_ref=power,
            dst_ref=power_all.at[group],
            send_sem=power_send.at[distance - 1],
            recv_sem=power_recv.at[distance - 1],
            device_id={"chan": lax.rem(group + distance, groups)},
            device_id_type=MESH,
        )
        copy.start()
        power_copies.append(copy)
    power_all[group] = power[...]
    for copy in (*halos, *filter_copies, *gated_copies, *result_copies):
        copy.wait_send()
    for copy in power_copies:
        copy.wait()
    power_out[...] = jnp.sum(power_all[...], axis=0)
    for copy in stores:
        copy.wait()


SLICES = 8


def normalize(channels, mixed_in, power, gain, out, mixed, scaled, scale, load_sem, store_sem):
    rows, width = mixed.shape
    count = rows // SLICES
    loads, stores = [], []
    for index in range(SLICES):
        at = pl.ds(index * count, count)
        loads.append(
            pltpu.make_async_copy(mixed_in.at[at, :], mixed.at[at, :], load_sem.at[index])
        )
        stores.append(
            pltpu.make_async_copy(scaled.at[at, :], out.at[at, :], store_sem.at[index])
        )
    for copy in loads:
        copy.start()
    row_scale = lax.rsqrt(power[pl.ds(0, 1), :] / channels + 1e-06)
    scale[...] = jnp.broadcast_to(row_scale, (LANES, rows)).T
    for index in range(SLICES):
        at = pl.ds(index * count, count)
        loads[index].wait()
        factor = scale[at, :]
        for start in range(0, width, LANES):
            lanes = pl.ds(start, LANES)
            scaled[at, lanes] = mixed[at, lanes] * factor * gain[:, lanes]
        stores[index].start()
    for copy in stores:
        copy.wait()


def fused(
    query_stream, key_stream, value_stream, short_filters, long_filter, skip_bias, norm_gain
):
    rows, width = query_stream.shape
    parts = lax.axis_size("seq")
    groups = lax.axis_size("chan")
    tokens = rows * parts
    part = width // parts
    forward, backward = tables(tokens, parts)
    dma = pltpu.SemaphoreType.DMA
    bf16, f32 = jnp.bfloat16, jnp.float32
    mixed, power = pl.pallas_call(
        functools.partial(kernel, parts, groups),
        out_shape=(
            jax.ShapeDtypeStruct((rows, width), f32),
            jax.ShapeDtypeStruct((8, rows), f32),
        ),
        in_specs=[pl.BlockSpec(memory_space=pl.ANY)] * 8,
        out_specs=(
            pl.BlockSpec(memory_space=pl.ANY),
            pl.BlockSpec(memory_space=pltpu.VMEM),
        ),
        scratch_shapes=[
            pltpu.VMEM((3, rows + PACK, width), bf16),
            pltpu.VMEM(short_filters.shape, f32),
            pltpu.VMEM((1, width), f32),
            pltpu.VMEM(forward.shape, bf16),
            pltpu.VMEM(backward.shape, bf16),
            pltpu.VMEM((parts, rows, part), bf16),
            pltpu.VMEM((parts, rows, part), bf16),
            pltpu.VMEM((parts, rows, part), bf16),
            pltpu.VMEM((parts, rows, part), bf16),
            pltpu.VMEM((rows, width), f32),
            pltpu.VMEM((2 * tokens, part), f32),
            pltpu.VMEM((2 * tokens, part), f32),
            pltpu.VMEM((2 * tokens, part), bf16),
            pltpu.VMEM((parts, rows, part), bf16),
            pltpu.VMEM((parts, rows, part), bf16),
            pltpu.VMEM((rows, width), f32),
            pltpu.VMEM((rows, LANES), f32),
            pltpu.VMEM((8, rows), f32),
            pltpu.VMEM((groups, 8, rows), f32),
            dma((8,)),
            dma((parts - 1,)),
            dma((3,)),
            dma((3,)),
            dma((parts - 1,)),
            dma((parts - 1,)),
            dma((parts - 1,)),
            dma((parts - 1,)),
            dma((parts - 1,)),
            dma((parts - 1,)),
            dma((groups - 1,)),
            dma((groups - 1,)),
            dma((parts,)),
        ],
        compiler_params=pltpu.CompilerParams(
            collective_id=0, has_side_effects=True, vmem_limit_bytes=VMEM_BYTES
        ),
    )(
        query_stream,
        key_stream,
        value_stream,
        short_filters,
        long_filter,
        skip_bias[None, :],
        jnp.asarray(forward),
        jnp.asarray(backward),
    )
    return pl.pallas_call(
        functools.partial(normalize, width * groups),
        out_shape=jax.ShapeDtypeStruct((rows, width), f32),
        in_specs=[
            pl.BlockSpec(memory_space=pl.ANY),
            pl.BlockSpec(memory_space=pltpu.VMEM),
            pl.BlockSpec(memory_space=pltpu.VMEM),
        ],
        out_specs=pl.BlockSpec(memory_space=pl.ANY),
        scratch_shapes=[
            pltpu.VMEM((rows, width), f32),
            pltpu.VMEM((rows, width), f32),
            pltpu.VMEM((rows, LANES), f32),
            dma((SLICES,)),
            dma((SLICES,)),
        ],
        compiler_params=pltpu.CompilerParams(vmem_limit_bytes=16 * 1024 * 1024),
    )(mixed, power, norm_gain[None, :])


def dense_fits(mesh, shape):
    tokens, channels = shape
    part = channels // (mesh.shape["chan"] * mesh.shape["seq"])
    rows = tokens // mesh.shape["seq"]
    return (
        part % LANES == 0
        and rows % 256 == 0
        and mesh.shape["seq"] > 1
        and mesh.shape["chan"] > 1
        and 8 * tokens * tokens <= VMEM_BYTES // 4
    )


def solution(mesh):
    placed = (
        P("seq", "chan"),
        P("seq", "chan"),
        P("seq", "chan"),
        P(None, None, "chan"),
        P("seq", "chan"),
        P("chan"),
        P("chan"),
    )

    def apply(query_stream, *others):
        body = fused if dense_fits(mesh, query_stream.shape) else shards
        return jax.shard_map(
            body, mesh=mesh, in_specs=placed, out_specs=P("seq", "chan"), check_vma=False
        )(query_stream, *others)

    return apply
```

```python
import functools
import math

import jax
import jax.numpy as jnp
import numpy as np
from jax import lax
from jax.experimental import pallas as pl
from jax.experimental.pallas import tpu as pltpu
from jax.sharding import PartitionSpec as P

D = 8192


def from_behind(value, axis, steps):
    count = lax.axis_size(axis)
    first, last = (max(0, -steps), min(count, count - steps))
    return lax.ppermute(value, axis, [(source, source + steps) for source in range(first, last)])


def rotation(first_index, second_index, period):
    product = first_index[:, None] * second_index[None, :] % period
    angle = product.astype(jnp.float32) * (2.0 * math.pi / period)
    return (jnp.cos(angle), jnp.sin(angle))


def halves(values):
    upper = values.astype(jnp.bfloat16)
    lower = (values - upper.astype(jnp.float32)).astype(jnp.bfloat16)
    return (upper, lower)


def mixing(table, operand, form):
    table_high, table_low = halves(table)
    if operand.dtype == jnp.bfloat16:
        pairs = [(table_high, operand), (table_low, operand)]
    else:
        operand_high, operand_low = halves(operand)
        pairs = [(table_high, operand_high), (table_low, operand_high), (table_high, operand_low)]
    total = None
    for left, right in pairs:
        term = jnp.einsum(form, left, right, preferred_element_type=jnp.float32)
        total = term if total is None else total + term
    return total


def swapped_convolution(gated, long_filter):
    block_rows, local_width = gated.shape
    seq_count = lax.axis_size("seq")
    full_length = 2 * seq_count * block_rows
    signal_in, filter_in = (
        lax.all_to_all(gated[:, None, :], "seq", split_axis=2, concat_axis=1, tiled=True),
        lax.all_to_all(long_filter[:, None, :], "seq", split_axis=2, concat_axis=1, tiled=True),
    )
    freq_short = jnp.arange(2 * seq_count, dtype=jnp.int32)
    cos_short, sin_short = rotation(
        freq_short, jnp.arange(seq_count, dtype=jnp.int32), 2 * seq_count
    )
    long_index = jnp.arange(block_rows, dtype=jnp.int32)
    cos_turn, sin_turn = rotation(long_index, freq_short, full_length)
    cos_turn = cos_turn[:, :, None]
    sin_turn = sin_turn[:, :, None]
    cos_long, sin_long = rotation(long_index, long_index, block_rows)

    def transform(signal):
        real_part = mixing(cos_short, signal, "km,jmc->jkc")
        imag_part = -mixing(sin_short, signal, "km,jmc->jkc")
        twisted_real = (real_part * cos_turn + imag_part * sin_turn).reshape(block_rows, -1)
        twisted_imag = (imag_part * cos_turn - real_part * sin_turn).reshape(block_rows, -1)
        out_real = mixing(cos_long, twisted_real, "kj,jc->kc") + mixing(
            sin_long, twisted_imag, "kj,jc->kc"
        )
        out_imag = mixing(cos_long, twisted_imag, "kj,jc->kc") - mixing(
            sin_long, twisted_real, "kj,jc->kc"
        )
        return (out_real, out_imag)

    signal_real, signal_imag = transform(signal_in)
    filter_real, filter_imag = transform(filter_in)
    prod_real = signal_real * filter_real - signal_imag * filter_imag
    prod_imag = signal_real * filter_imag + signal_imag * filter_real
    back_real = mixing(cos_long, prod_real, "kj,jc->kc") - mixing(sin_long, prod_imag, "kj,jc->kc")
    back_imag = mixing(sin_long, prod_real, "kj,jc->kc") + mixing(cos_long, prod_imag, "kj,jc->kc")
    back_real = back_real.reshape(block_rows, 2 * seq_count, -1)
    back_imag = back_imag.reshape(block_rows, 2 * seq_count, -1)
    turned_real = back_real * cos_turn - back_imag * sin_turn
    turned_imag = back_real * sin_turn + back_imag * cos_turn
    result = (
        mixing(cos_short.T, turned_real, "mk,jkc->jmc")
        - mixing(sin_short.T, turned_imag, "mk,jkc->jmc")
    ) / full_length
    gathered = lax.all_to_all(result, "seq", split_axis=1, concat_axis=2, tiled=True)
    return gathered.reshape(block_rows, local_width)


def shards(
    query_stream, key_stream, value_stream, short_filters, long_filter, skip_bias, norm_gain
):
    block_rows = query_stream.shape[0]
    tap_count = short_filters.shape[1]
    stacked = jnp.stack([query_stream, key_stream, value_stream])
    previous = from_behind(stacked[:, block_rows - tap_count + 1 :, :], "seq", 1)
    extended = jnp.concatenate([previous, stacked], axis=1).astype(jnp.float32)
    convolved = jnp.zeros(stacked.shape, jnp.float32)
    for offset in range(tap_count):
        start = tap_count - 1 - offset
        convolved = (
            convolved
            + short_filters[:, offset, None, :] * extended[:, start : start + block_rows, :]
        )
    query_conv = convolved[0]
    gated = (convolved[1] * convolved[2]).astype(jnp.bfloat16)
    long_out = swapped_convolution(gated, long_filter)
    mixed = jax.nn.silu(query_conv * (long_out + skip_bias[None, :] * gated.astype(jnp.float32)))
    row_power = lax.psum(jnp.sum(mixed * mixed, axis=1), "chan")
    return mixed * lax.rsqrt(row_power / D + 1e-06)[:, None] * norm_gain[None, :]


MESH = pl.DeviceIdType.MESH
PACK = 16
LANES = 128
VMEM_BYTES = 60 * 1024 * 1024


def tables(tokens, parts):
    freq = 2 * np.arange(tokens, dtype=np.int64) + 1
    time = np.arange(tokens, dtype=np.int64)
    angle = (freq[:, None] * time[None, :] % (4 * tokens)) * (2.0 * np.pi / (4 * tokens))
    forward = np.concatenate([np.cos(angle), -np.sin(angle)], axis=0)
    backward = forward.T / tokens
    rows = tokens // parts
    forward = forward.reshape(2 * tokens, parts, rows).transpose(1, 0, 2)
    backward = backward.reshape(parts, rows, 2 * tokens)
    return (forward.astype(jnp.bfloat16), backward.astype(jnp.bfloat16))


def kernel(
    parts,
    groups,
    query,
    key,
    value,
    taps_in,
    filt,
    skip_in,
    forward_in,
    backward_in,
    mixed,
    power_out,
    extended,
    taps,
    skip,
    forward,
    backward,
    filter_stage,
    filter_all,
    gated,
    gated_all,
    query_conv,
    spectrum,
    filter_spectrum,
    product,
    result,
    result_all,
    partial,
    power,
    power_all,
    load_sem,
    stage_sem,
    halo_send,
    halo_recv,
    filter_send,
    filter_recv,
    gated_send,
    gated_recv,
    result_send,
    result_recv,
    power_send,
    power_recv,
):
    me = lax.axis_index("seq")
    group = lax.axis_index("chan")
    rows, width = mixed.shape
    part = width // parts
    tokens = rows * parts
    tap_count = taps.shape[1]

    def columns(owner):
        return pl.ds(pl.multiple_of(owner * part, LANES), part)

    def peer(distance):
        return lax.rem(me + distance, parts)

    def source(distance):
        return lax.rem(me + parts - distance, parts)

    streams = (key, value, query)
    loads = []
    for index, (src, dst) in enumerate(
        (
            (key, extended.at[0, pl.ds(PACK, rows), :]),
            (value, extended.at[1, pl.ds(PACK, rows), :]),
            (taps_in, taps),
            (query, extended.at[2, pl.ds(PACK, rows), :]),
            (filt.at[:, columns(me)], filter_all.at[me]),
            (forward_in, forward),
            (skip_in, skip),
            (backward_in, backward),
        )
    ):
        loads.append(pltpu.make_async_copy(src, dst, load_sem.at[index]))
    staged = [
        pltpu.make_async_copy(
            filt.at[:, columns(peer(d))], filter_stage.at[peer(d)], stage_sem.at[d - 1]
        )
        for d in range(1, parts)
    ]
    for copy in (*staged, *loads[:5]):
        copy.start()

    barrier = pltpu.get_barrier_semaphore()
    for distance in range(1, parts):
        pl.semaphore_signal(
            barrier, inc=1, device_id={"seq": peer(distance)}, device_id_type=MESH
        )
    for distance in range(1, groups):
        pl.semaphore_signal(
            barrier,
            inc=1,
            device_id={"chan": lax.rem(group + distance, groups)},
            device_id_type=MESH,
        )
    pl.semaphore_wait(barrier, parts + groups - 2)

    halos = []
    for index in range(3):
        copy = pltpu.make_async_remote_copy(
            src_ref=streams[index].at[pl.ds(rows - PACK, PACK), :],
            dst_ref=extended.at[index, pl.ds(0, PACK), :],
            send_sem=halo_send.at[index],
            recv_sem=halo_recv.at[index],
            device_id={"seq": peer(1)},
            device_id_type=MESH,
        )
        copy.start()
        halos.append(copy)

    def exchange(src, dst, send_sem, recv_sem, distance):
        copy = pltpu.make_async_remote_copy(
            src_ref=src,
            dst_ref=dst.at[me],
            send_sem=send_sem.at[distance - 1],
            recv_sem=recv_sem.at[distance - 1],
            device_id={"seq": peer(distance)},
            device_id_type=MESH,
        )
        copy.start()
        return copy

    filter_copies = []
    for d in range(1, parts):
        staged[d - 1].wait()
        filter_copies.append(
            exchange(filter_stage.at[peer(d)], filter_all, filter_send, filter_recv, d)
        )
    for copy in loads[5:]:
        copy.start()

    def ready(index):
        halos[index].wait_recv()

        @pl.when(me == 0)
        def _():
            extended[index, pl.ds(0, PACK), :] = jnp.zeros((PACK, width), extended.dtype)

    block = 64
    tiles = part // LANES

    def short(index, weight, start, lanes):
        window = extended[index, pl.ds(start, block + PACK), lanes].astype(jnp.float32)
        stride = min(4, tap_count)
        shifted = [window] + [
            pltpu.roll(window, first, 0) for first in range(stride, tap_count, stride)
        ]
        total = None
        for b in reversed(range(stride)):
            if total is not None:
                total = pltpu.roll(total, 1, 0)
            for a, held in enumerate(shifted):
                tap = a * stride + b
                if tap < tap_count:
                    term = taps[weight, pl.ds(tap, 1), lanes] * held
                    total = term if total is None else total + term
        return total[PACK:]

    for index in range(3):
        loads[index].wait()

    def gate(tile_at, start):
        lanes = pl.ds(pl.multiple_of(tile_at * LANES, LANES), LANES)
        gated[tile_at // tiles, tile_at % tiles, pl.ds(start, block), :] = (
            short(0, 1, start, lanes) * short(1, 2, start, lanes)
        ).astype(gated.dtype)

    inner_blocks = rows // block - 1

    def gate_inner(step, _):
        gate(step // inner_blocks, pl.multiple_of((step % inner_blocks + 1) * block, block))
        return 0

    lax.fori_loop(0, parts * tiles * inner_blocks, gate_inner, 0)
    ready(0)
    ready(1)
    gated_copies = [[] for _ in range(tiles)]
    for group_at in range(tiles):
        for d in (*range(1, parts), 0):
            owner = peer(d)
            gate(owner * tiles + group_at, 0)
            if d:
                gated_copies[group_at].append(
                    exchange(
                        gated.at[owner, group_at],
                        gated_all.at[group_at],
                        gated_send.at[group_at],
                        gated_recv.at[group_at],
                        d,
                    )
                )

    loads[3].wait()
    ready(2)

    def query_step(step, _):
        start = pl.multiple_of(step // (width // LANES) * block, block)
        lanes = pl.ds(pl.multiple_of(step % (width // LANES) * LANES, LANES), LANES)
        query_conv[pl.ds(start, block), lanes] = short(2, 0, start, lanes)
        return 0

    lax.fori_loop(0, rows // block * (width // LANES), query_step, 0)

    loads[4].wait()
    loads[5].wait()
    for copy in filter_copies:
        copy.wait_recv()
    tile = 256

    def filter_step(step, _):
        at = pl.ds(pl.multiple_of(step * tile, tile), tile)
        total = None
        for j in range(parts):
            term = jnp.dot(
                forward[j, at, :], filter_all[j], preferred_element_type=jnp.float32
            )
            total = term if total is None else total + term
        filter_spectrum[at, :] = total
        return 0

    lax.fori_loop(0, 2 * tokens // tile, filter_step, 0)

    wide = 512

    def accumulate(owner, operand, first):
        def step_body(step, _):
            at = pl.ds(pl.multiple_of(step * wide, wide), wide)
            term = jnp.dot(forward[owner, at, :], operand(), preferred_element_type=jnp.float32)
            spectrum[at, :] = term if first else spectrum[at, :] + term
            return 0

        lax.fori_loop(0, 2 * tokens // wide, step_body, 0)

    result_copies = [[] for _ in range(tiles)]
    for group_at in range(tiles):
        accumulate(me, lambda: gated[me, group_at], True)
        for d in range(1, parts):
            gated_copies[group_at][d - 1].wait_recv()
            owner = source(d)
            accumulate(owner, lambda: gated_all[group_at, owner], False)
        group_lanes = pl.ds(group_at * LANES, LANES)

        def product_step(step, _):
            real = pl.ds(pl.multiple_of(step * block, block), block)
            imag = pl.ds(pl.multiple_of(tokens + step * block, block), block)
            a, b = spectrum[real, :], spectrum[imag, :]
            c, d = filter_spectrum[real, group_lanes], filter_spectrum[imag, group_lanes]
            product[real, :] = (a * c - b * d).astype(product.dtype)
            product[imag, :] = (a * d + b * c).astype(product.dtype)
            return 0

        lax.fori_loop(0, tokens // block, product_step, 0)
        if group_at == 0:
            loads[7].wait()
        for d in (*range(1, parts), 0):
            owner = peer(d)
            result[group_at, owner] = jnp.dot(
                backward[owner], product[...], preferred_element_type=jnp.float32
            ).astype(result.dtype)
            if d:
                result_copies[group_at].append(
                    exchange(
                        result.at[group_at, owner],
                        result_all.at[group_at],
                        result_send.at[group_at],
                        result_recv.at[group_at],
                        d,
                    )
                )

    loads[6].wait()
    partial[...] = jnp.zeros_like(partial)

    def finish(owner, group_at, held):
        lanes = pl.ds(pl.multiple_of(owner * part + group_at * LANES, LANES), LANES)

        def step_body(step, _):
            at = pl.ds(pl.multiple_of(step * block, block), block)
            long_out = held[group_at, owner, at, :].astype(jnp.float32)
            direct = skip[:, lanes] * gated[owner, group_at, at, :].astype(jnp.float32)
            x = query_conv[at, lanes] * (long_out + direct)
            y = x / (1.0 + jnp.exp(-x))
            mixed[at, lanes] = y
            partial[at, :] = partial[at, :] + y * y
            return 0

        lax.fori_loop(0, rows // block, step_body, 0)

    for group_at in range(tiles):
        finish(me, group_at, result)
        for d in range(1, parts):
            result_copies[group_at][d - 1].wait_recv()
            finish(source(d), group_at, result_all)

    power[...] = jnp.broadcast_to(
        jnp.sum(partial[...].T, axis=0, keepdims=True), power.shape
    )
    power_copies = []
    for distance in range(1, groups):
        copy = pltpu.make_async_remote_copy(
            src_ref=power,
            dst_ref=power_all.at[group],
            send_sem=power_send.at[distance - 1],
            recv_sem=power_recv.at[distance - 1],
            device_id={"chan": lax.rem(group + distance, groups)},
            device_id_type=MESH,
        )
        copy.start()
        power_copies.append(copy)
    power_all[group] = power[...]
    for copy in (*halos, *filter_copies, *sum(gated_copies + result_copies, [])):
        copy.wait_send()
    for copy in power_copies:
        copy.wait()
    power_out[...] = jnp.sum(power_all[...], axis=0)


SLICES = 8


def normalize(channels, mixed, power, gain, out, scaled, scale, store_sem):
    rows, width = mixed.shape
    count = rows // SLICES
    row_scale = lax.rsqrt(power[pl.ds(0, 1), :] / channels + 1e-06)
    scale[...] = jnp.broadcast_to(row_scale, (LANES, rows)).T
    stores = []
    for index in range(SLICES):
        at = pl.ds(index * count, count)
        factor = scale[at, :]
        for start in range(0, width, LANES):
            lanes = pl.ds(start, LANES)
            scaled[at, lanes] = mixed[at, lanes] * factor * gain[:, lanes]
        copy = pltpu.make_async_copy(scaled.at[at, :], out.at[at, :], store_sem.at[index])
        copy.start()
        stores.append(copy)
    for copy in stores:
        copy.wait()


def fused(
    query_stream, key_stream, value_stream, short_filters, long_filter, skip_bias, norm_gain
):
    rows, width = query_stream.shape
    parts = lax.axis_size("seq")
    groups = lax.axis_size("chan")
    tokens = rows * parts
    part = width // parts
    tiles = part // LANES
    forward, backward = tables(tokens, parts)
    dma = pltpu.SemaphoreType.DMA
    bf16, f32 = jnp.bfloat16, jnp.float32
    mixed, power = pl.pallas_call(
        functools.partial(kernel, parts, groups),
        out_shape=(pltpu.VMEM((rows, width), f32), pltpu.VMEM((8, rows), f32)),
        in_specs=[pl.BlockSpec(memory_space=pl.ANY)] * 8,
        out_specs=(
            pl.BlockSpec(memory_space=pltpu.VMEM),
            pl.BlockSpec(memory_space=pltpu.VMEM),
        ),
        scratch_shapes=[
            pltpu.VMEM((3, rows + PACK, width), bf16),
            pltpu.VMEM(short_filters.shape, f32),
            pltpu.VMEM((1, width), f32),
            pltpu.VMEM(forward.shape, bf16),
            pltpu.VMEM(backward.shape, bf16),
            pltpu.VMEM((parts, rows, part), bf16),
            pltpu.VMEM((parts, rows, part), bf16),
            pltpu.VMEM((parts, tiles, rows, LANES), bf16),
            pltpu.VMEM((tiles, parts, rows, LANES), bf16),
            pltpu.VMEM((rows, width), f32),
            pltpu.VMEM((2 * tokens, LANES), f32),
            pltpu.VMEM((2 * tokens, part), f32),
            pltpu.VMEM((2 * tokens, LANES), bf16),
            pltpu.VMEM((tiles, parts, rows, LANES), bf16),
            pltpu.VMEM((tiles, parts, rows, LANES), bf16),
            pltpu.VMEM((rows, LANES), f32),
            pltpu.VMEM((8, rows), f32),
            pltpu.VMEM((groups, 8, rows), f32),
            dma((8,)),
            dma((parts - 1,)),
            dma((3,)),
            dma((3,)),
            dma((parts - 1,)),
            dma((parts - 1,)),
            dma((tiles, parts - 1)),
            dma((tiles, parts - 1)),
            dma((tiles, parts - 1)),
            dma((tiles, parts - 1)),
            dma((groups - 1,)),
            dma((groups - 1,)),
        ],
        compiler_params=pltpu.CompilerParams(
            collective_id=0, has_side_effects=True, vmem_limit_bytes=VMEM_BYTES
        ),
    )(
        query_stream,
        key_stream,
        value_stream,
        short_filters,
        long_filter,
        skip_bias[None, :],
        jnp.asarray(forward),
        jnp.asarray(backward),
    )
    return pl.pallas_call(
        functools.partial(normalize, width * groups),
        out_shape=jax.ShapeDtypeStruct((rows, width), f32),
        in_specs=[pl.BlockSpec(memory_space=pltpu.VMEM)] * 3,
        out_specs=pl.BlockSpec(memory_space=pl.ANY),
        scratch_shapes=[
            pltpu.VMEM((rows, width), f32),
            pltpu.VMEM((rows, LANES), f32),
            dma((SLICES,)),
        ],
        compiler_params=pltpu.CompilerParams(vmem_limit_bytes=16 * 1024 * 1024),
    )(mixed, power, norm_gain[None, :])


def dense_fits(mesh, shape):
    tokens, channels = shape
    part = channels // (mesh.shape["chan"] * mesh.shape["seq"])
    rows = tokens // mesh.shape["seq"]
    return (
        part % LANES == 0
        and rows % 256 == 0
        and mesh.shape["seq"] > 1
        and mesh.shape["chan"] > 1
        and 8 * tokens * tokens <= VMEM_BYTES // 4
    )


def solution(mesh):
    placed = (
        P("seq", "chan"),
        P("seq", "chan"),
        P("seq", "chan"),
        P(None, None, "chan"),
        P("seq", "chan"),
        P("chan"),
        P("chan"),
    )

    def apply(query_stream, *others):
        body = fused if dense_fits(mesh, query_stream.shape) else shards
        return jax.shard_map(
            body, mesh=mesh, in_specs=placed, out_specs=P("seq", "chan"), check_vma=False
        )(query_stream, *others)

    return apply
```

```python
import functools
import math

import jax
import jax.numpy as jnp
import numpy as np
from jax import lax
from jax.experimental import pallas as pl
from jax.experimental.pallas import tpu as pltpu
from jax.sharding import PartitionSpec as P

D = 8192


def from_behind(value, axis, steps):
    count = lax.axis_size(axis)
    first, last = (max(0, -steps), min(count, count - steps))
    return lax.ppermute(value, axis, [(source, source + steps) for source in range(first, last)])


def rotation(first_index, second_index, period):
    product = first_index[:, None] * second_index[None, :] % period
    angle = product.astype(jnp.float32) * (2.0 * math.pi / period)
    return (jnp.cos(angle), jnp.sin(angle))


def halves(values):
    upper = values.astype(jnp.bfloat16)
    lower = (values - upper.astype(jnp.float32)).astype(jnp.bfloat16)
    return (upper, lower)


def mixing(table, operand, form):
    table_high, table_low = halves(table)
    if operand.dtype == jnp.bfloat16:
        pairs = [(table_high, operand), (table_low, operand)]
    else:
        operand_high, operand_low = halves(operand)
        pairs = [(table_high, operand_high), (table_low, operand_high), (table_high, operand_low)]
    total = None
    for left, right in pairs:
        term = jnp.einsum(form, left, right, preferred_element_type=jnp.float32)
        total = term if total is None else total + term
    return total


def swapped_convolution(gated, long_filter):
    block_rows, local_width = gated.shape
    seq_count = lax.axis_size("seq")
    full_length = 2 * seq_count * block_rows
    signal_in, filter_in = (
        lax.all_to_all(gated[:, None, :], "seq", split_axis=2, concat_axis=1, tiled=True),
        lax.all_to_all(long_filter[:, None, :], "seq", split_axis=2, concat_axis=1, tiled=True),
    )
    freq_short = jnp.arange(2 * seq_count, dtype=jnp.int32)
    cos_short, sin_short = rotation(
        freq_short, jnp.arange(seq_count, dtype=jnp.int32), 2 * seq_count
    )
    long_index = jnp.arange(block_rows, dtype=jnp.int32)
    cos_turn, sin_turn = rotation(long_index, freq_short, full_length)
    cos_turn = cos_turn[:, :, None]
    sin_turn = sin_turn[:, :, None]
    cos_long, sin_long = rotation(long_index, long_index, block_rows)

    def transform(signal):
        real_part = mixing(cos_short, signal, "km,jmc->jkc")
        imag_part = -mixing(sin_short, signal, "km,jmc->jkc")
        twisted_real = (real_part * cos_turn + imag_part * sin_turn).reshape(block_rows, -1)
        twisted_imag = (imag_part * cos_turn - real_part * sin_turn).reshape(block_rows, -1)
        out_real = mixing(cos_long, twisted_real, "kj,jc->kc") + mixing(
            sin_long, twisted_imag, "kj,jc->kc"
        )
        out_imag = mixing(cos_long, twisted_imag, "kj,jc->kc") - mixing(
            sin_long, twisted_real, "kj,jc->kc"
        )
        return (out_real, out_imag)

    signal_real, signal_imag = transform(signal_in)
    filter_real, filter_imag = transform(filter_in)
    prod_real = signal_real * filter_real - signal_imag * filter_imag
    prod_imag = signal_real * filter_imag + signal_imag * filter_real
    back_real = mixing(cos_long, prod_real, "kj,jc->kc") - mixing(sin_long, prod_imag, "kj,jc->kc")
    back_imag = mixing(sin_long, prod_real, "kj,jc->kc") + mixing(cos_long, prod_imag, "kj,jc->kc")
    back_real = back_real.reshape(block_rows, 2 * seq_count, -1)
    back_imag = back_imag.reshape(block_rows, 2 * seq_count, -1)
    turned_real = back_real * cos_turn - back_imag * sin_turn
    turned_imag = back_real * sin_turn + back_imag * cos_turn
    result = (
        mixing(cos_short.T, turned_real, "mk,jkc->jmc")
        - mixing(sin_short.T, turned_imag, "mk,jkc->jmc")
    ) / full_length
    gathered = lax.all_to_all(result, "seq", split_axis=1, concat_axis=2, tiled=True)
    return gathered.reshape(block_rows, local_width)


def shards(
    query_stream, key_stream, value_stream, short_filters, long_filter, skip_bias, norm_gain
):
    block_rows = query_stream.shape[0]
    tap_count = short_filters.shape[1]
    stacked = jnp.stack([query_stream, key_stream, value_stream])
    previous = from_behind(stacked[:, block_rows - tap_count + 1 :, :], "seq", 1)
    extended = jnp.concatenate([previous, stacked], axis=1).astype(jnp.float32)
    convolved = jnp.zeros(stacked.shape, jnp.float32)
    for offset in range(tap_count):
        start = tap_count - 1 - offset
        convolved = (
            convolved
            + short_filters[:, offset, None, :] * extended[:, start : start + block_rows, :]
        )
    query_conv = convolved[0]
    gated = (convolved[1] * convolved[2]).astype(jnp.bfloat16)
    long_out = swapped_convolution(gated, long_filter)
    mixed = jax.nn.silu(query_conv * (long_out + skip_bias[None, :] * gated.astype(jnp.float32)))
    row_power = lax.psum(jnp.sum(mixed * mixed, axis=1), "chan")
    return mixed * lax.rsqrt(row_power / D + 1e-06)[:, None] * norm_gain[None, :]


MESH = pl.DeviceIdType.MESH
PACK = 16
LANES = 128
VMEM_BYTES = 60 * 1024 * 1024


def tables(tokens, parts):
    freq = 2 * np.arange(tokens, dtype=np.int64) + 1
    time = np.arange(tokens, dtype=np.int64)
    angle = (freq[:, None] * time[None, :] % (4 * tokens)) * (2.0 * np.pi / (4 * tokens))
    forward = np.concatenate([np.cos(angle), -np.sin(angle)], axis=0)
    backward = forward.T / tokens
    rows = tokens // parts
    backward = backward.reshape(parts, rows, 2 * tokens)
    return (forward.astype(jnp.bfloat16), backward.astype(jnp.bfloat16))


def kernel(
    parts,
    groups,
    query,
    key,
    value,
    taps_in,
    filt,
    skip_in,
    forward_in,
    backward_in,
    mixed,
    power_out,
    extended,
    taps,
    skip,
    forward,
    backward,
    filter_stage,
    filter_all,
    gated,
    gated_all,
    query_conv,
    filter_spectrum,
    product,
    result,
    result_all,
    partial,
    power,
    power_all,
    load_sem,
    stage_sem,
    halo_send,
    halo_recv,
    filter_send,
    filter_recv,
    gated_send,
    gated_recv,
    result_send,
    result_recv,
    power_send,
    power_recv,
):
    me = lax.axis_index("seq")
    group = lax.axis_index("chan")
    rows, width = mixed.shape
    part = width // parts
    tokens = rows * parts
    tap_count = taps.shape[1]

    def columns(owner):
        return pl.ds(pl.multiple_of(owner * part, LANES), part)

    def peer(distance):
        return lax.rem(me + distance, parts)

    def source(distance):
        return lax.rem(me + parts - distance, parts)

    streams = (key, value, query)
    loads = []
    for index, (src, dst) in enumerate(
        (
            (key, extended.at[0, pl.ds(PACK, rows), :]),
            (value, extended.at[1, pl.ds(PACK, rows), :]),
            (taps_in, taps),
            (query, extended.at[2, pl.ds(PACK, rows), :]),
            (filt.at[:, columns(me)], filter_all.at[me]),
            (forward_in, forward),
            (skip_in, skip),
            (backward_in, backward),
        )
    ):
        loads.append(pltpu.make_async_copy(src, dst, load_sem.at[index]))
    staged = [
        pltpu.make_async_copy(
            filt.at[:, columns(peer(d))], filter_stage.at[peer(d)], stage_sem.at[d - 1]
        )
        for d in range(1, parts)
    ]
    for copy in (*staged, *loads[:5]):
        copy.start()

    barrier = pltpu.get_barrier_semaphore()
    for distance in range(1, parts):
        pl.semaphore_signal(
            barrier, inc=1, device_id={"seq": peer(distance)}, device_id_type=MESH
        )
    for distance in range(1, groups):
        pl.semaphore_signal(
            barrier,
            inc=1,
            device_id={"chan": lax.rem(group + distance, groups)},
            device_id_type=MESH,
        )
    pl.semaphore_wait(barrier, parts + groups - 2)

    halos = []
    for index in range(3):
        copy = pltpu.make_async_remote_copy(
            src_ref=streams[index].at[pl.ds(rows - PACK, PACK), :],
            dst_ref=extended.at[index, pl.ds(0, PACK), :],
            send_sem=halo_send.at[index],
            recv_sem=halo_recv.at[index],
            device_id={"seq": peer(1)},
            device_id_type=MESH,
        )
        copy.start()
        halos.append(copy)

    def exchange(src, dst, send_sem, recv_sem, distance):
        copy = pltpu.make_async_remote_copy(
            src_ref=src,
            dst_ref=dst.at[me],
            send_sem=send_sem.at[distance - 1],
            recv_sem=recv_sem.at[distance - 1],
            device_id={"seq": peer(distance)},
            device_id_type=MESH,
        )
        copy.start()
        return copy

    filter_copies = []
    for d in range(1, parts):
        staged[d - 1].wait()
        filter_copies.append(
            exchange(filter_stage.at[peer(d)], filter_all, filter_send, filter_recv, d)
        )
    for copy in loads[5:]:
        copy.start()

    def ready(index):
        halos[index].wait_recv()

        @pl.when(me == 0)
        def _():
            extended[index, pl.ds(0, PACK), :] = jnp.zeros((PACK, width), extended.dtype)

    block = 64
    tiles = part // LANES

    def short(index, weight, start, lanes):
        window = extended[index, pl.ds(start, block + PACK), lanes].astype(jnp.float32)
        stride = min(4, tap_count)
        shifted = [window] + [
            pltpu.roll(window, first, 0) for first in range(stride, tap_count, stride)
        ]
        total = None
        for b in reversed(range(stride)):
            if total is not None:
                total = pltpu.roll(total, 1, 0)
            for a, held in enumerate(shifted):
                tap = a * stride + b
                if tap < tap_count:
                    term = taps[weight, pl.ds(tap, 1), lanes] * held
                    total = term if total is None else total + term
        return total[PACK:]

    for index in range(3):
        loads[index].wait()

    def gate(tile_at, start):
        lanes = pl.ds(pl.multiple_of(tile_at * LANES, LANES), LANES)
        inner = pl.ds(pl.multiple_of(tile_at % tiles * LANES, LANES), LANES)
        gated[tile_at // tiles, pl.ds(start, block), inner] = (
            short(0, 1, start, lanes) * short(1, 2, start, lanes)
        ).astype(gated.dtype)

    inner_blocks = rows // block - 1

    def gate_inner(step, _):
        gate(step // inner_blocks, pl.multiple_of((step % inner_blocks + 1) * block, block))
        return 0

    lax.fori_loop(0, parts * tiles * inner_blocks, gate_inner, 0)
    ready(0)
    ready(1)
    gated_copies = []
    for d in (*range(1, parts), 0):
        owner = peer(d)
        for tile_at in range(tiles):
            gate(owner * tiles + tile_at, 0)
        if d:
            gated_copies.append(
                exchange(gated.at[owner], gated_all, gated_send, gated_recv, d)
            )
    gated_all[me] = gated[me]

    loads[3].wait()
    ready(2)

    def query_step(step, _):
        start = pl.multiple_of(step // (width // LANES) * block, block)
        lanes = pl.ds(pl.multiple_of(step % (width // LANES) * LANES, LANES), LANES)
        query_conv[pl.ds(start, block), lanes] = short(2, 0, start, lanes)
        return 0

    lax.fori_loop(0, rows // block * (width // LANES), query_step, 0)

    loads[4].wait()
    loads[5].wait()
    for copy in filter_copies:
        copy.wait_recv()
    tile = 256

    def transform(first, held):
        return jnp.dot(
            forward[pl.ds(first, tile), :],
            held[...].reshape(tokens, part),
            preferred_element_type=jnp.float32,
        )

    for first in range(0, 2 * tokens, tile):
        filter_spectrum[pl.ds(first, tile), :] = transform(first, filter_all)

    for copy in gated_copies:
        copy.wait_recv()
    for first in range(0, tokens, tile):
        real, imag = pl.ds(first, tile), pl.ds(tokens + first, tile)
        a, b = transform(first, gated_all), transform(tokens + first, gated_all)
        c, d = filter_spectrum[real, :], filter_spectrum[imag, :]
        product[real, :] = (a * c - b * d).astype(product.dtype)
        product[imag, :] = (a * d + b * c).astype(product.dtype)

    loads[7].wait()
    result_copies = []
    for d in (*range(1, parts), 0):
        owner = peer(d)
        result[owner] = jnp.dot(
            backward[owner], product[...], preferred_element_type=jnp.float32
        ).astype(result.dtype)
        if d:
            result_copies.append(
                exchange(result.at[owner], result_all, result_send, result_recv, d)
            )

    loads[6].wait()
    partial[...] = jnp.zeros_like(partial)

    def finish(owner, held):
        def step_body(step, _):
            at = pl.ds(pl.multiple_of(step // tiles * block, block), block)
            offset = step % tiles * LANES
            inner = pl.ds(pl.multiple_of(offset, LANES), LANES)
            lanes = pl.ds(pl.multiple_of(owner * part + offset, LANES), LANES)
            long_out = held[owner, at, inner].astype(jnp.float32)
            direct = skip[:, lanes] * gated[owner, at, inner].astype(jnp.float32)
            x = query_conv[at, lanes] * (long_out + direct)
            y = x / (1.0 + jnp.exp(-x))
            mixed[at, lanes] = y
            partial[at, :] = partial[at, :] + y * y
            return 0

        lax.fori_loop(0, rows // block * tiles, step_body, 0)

    finish(me, result)
    for d in range(1, parts):
        result_copies[d - 1].wait_recv()
        finish(source(d), result_all)

    power[...] = jnp.broadcast_to(
        jnp.sum(partial[...].T, axis=0, keepdims=True), power.shape
    )
    power_copies = []
    for distance in range(1, groups):
        copy = pltpu.make_async_remote_copy(
            src_ref=power,
            dst_ref=power_all.at[group],
            send_sem=power_send.at[distance - 1],
            recv_sem=power_recv.at[distance - 1],
            device_id={"chan": lax.rem(group + distance, groups)},
            device_id_type=MESH,
        )
        copy.start()
        power_copies.append(copy)
    power_all[group] = power[...]
    for copy in (*halos, *filter_copies, *gated_copies, *result_copies):
        copy.wait_send()
    for copy in power_copies:
        copy.wait()
    power_out[...] = jnp.sum(power_all[...], axis=0)


SLICES = 8


def normalize(channels, mixed, power, gain, out, scaled, scale, store_sem):
    rows, width = mixed.shape
    count = rows // SLICES
    row_scale = lax.rsqrt(power[pl.ds(0, 1), :] / channels + 1e-06)
    scale[...] = jnp.broadcast_to(row_scale, (LANES, rows)).T
    stores = []
    for index in range(SLICES):
        at = pl.ds(index * count, count)
        factor = scale[at, :]
        for start in range(0, width, LANES):
            lanes = pl.ds(start, LANES)
            scaled[at, lanes] = mixed[at, lanes] * factor * gain[:, lanes]
        copy = pltpu.make_async_copy(scaled.at[at, :], out.at[at, :], store_sem.at[index])
        copy.start()
        stores.append(copy)
    for copy in stores:
        copy.wait()


def fused(
    query_stream, key_stream, value_stream, short_filters, long_filter, skip_bias, norm_gain
):
    rows, width = query_stream.shape
    parts = lax.axis_size("seq")
    groups = lax.axis_size("chan")
    tokens = rows * parts
    part = width // parts
    forward, backward = tables(tokens, parts)
    dma = pltpu.SemaphoreType.DMA
    bf16, f32 = jnp.bfloat16, jnp.float32
    mixed, power = pl.pallas_call(
        functools.partial(kernel, parts, groups),
        out_shape=(pltpu.VMEM((rows, width), f32), pltpu.VMEM((8, rows), f32)),
        in_specs=[pl.BlockSpec(memory_space=pl.ANY)] * 8,
        out_specs=(
            pl.BlockSpec(memory_space=pltpu.VMEM),
            pl.BlockSpec(memory_space=pltpu.VMEM),
        ),
        scratch_shapes=[
            pltpu.VMEM((3, rows + PACK, width), bf16),
            pltpu.VMEM(short_filters.shape, f32),
            pltpu.VMEM((1, width), f32),
            pltpu.VMEM(forward.shape, bf16),
            pltpu.VMEM(backward.shape, bf16),
            pltpu.VMEM((parts, rows, part), bf16),
            pltpu.VMEM((parts, rows, part), bf16),
            pltpu.VMEM((parts, rows, part), bf16),
            pltpu.VMEM((parts, rows, part), bf16),
            pltpu.VMEM((rows, width), f32),
            pltpu.VMEM((2 * tokens, part), f32),
            pltpu.VMEM((2 * tokens, part), bf16),
            pltpu.VMEM((parts, rows, part), bf16),
            pltpu.VMEM((parts, rows, part), bf16),
            pltpu.VMEM((rows, LANES), f32),
            pltpu.VMEM((8, rows), f32),
            pltpu.VMEM((groups, 8, rows), f32),
            dma((8,)),
            dma((parts - 1,)),
            dma((3,)),
            dma((3,)),
            dma((parts - 1,)),
            dma((parts - 1,)),
            dma((parts - 1,)),
            dma((parts - 1,)),
            dma((parts - 1,)),
            dma((parts - 1,)),
            dma((groups - 1,)),
            dma((groups - 1,)),
        ],
        compiler_params=pltpu.CompilerParams(
            collective_id=0, has_side_effects=True, vmem_limit_bytes=VMEM_BYTES
        ),
    )(
        query_stream,
        key_stream,
        value_stream,
        short_filters,
        long_filter,
        skip_bias[None, :],
        jnp.asarray(forward),
        jnp.asarray(backward),
    )
    return pl.pallas_call(
        functools.partial(normalize, width * groups),
        out_shape=jax.ShapeDtypeStruct((rows, width), f32),
        in_specs=[pl.BlockSpec(memory_space=pltpu.VMEM)] * 3,
        out_specs=pl.BlockSpec(memory_space=pl.ANY),
        scratch_shapes=[
            pltpu.VMEM((rows, width), f32),
            pltpu.VMEM((rows, LANES), f32),
            dma((SLICES,)),
        ],
        compiler_params=pltpu.CompilerParams(vmem_limit_bytes=16 * 1024 * 1024),
    )(mixed, power, norm_gain[None, :])


def dense_fits(mesh, shape):
    tokens, channels = shape
    part = channels // (mesh.shape["chan"] * mesh.shape["seq"])
    rows = tokens // mesh.shape["seq"]
    return (
        part % LANES == 0
        and rows % 256 == 0
        and mesh.shape["seq"] > 1
        and mesh.shape["chan"] > 1
        and 8 * tokens * tokens <= VMEM_BYTES // 4
    )


def solution(mesh):
    placed = (
        P("seq", "chan"),
        P("seq", "chan"),
        P("seq", "chan"),
        P(None, None, "chan"),
        P("seq", "chan"),
        P("chan"),
        P("chan"),
    )

    def apply(query_stream, *others):
        body = fused if dense_fits(mesh, query_stream.shape) else shards
        return jax.shard_map(
            body, mesh=mesh, in_specs=placed, out_specs=P("seq", "chan"), check_vma=False
        )(query_stream, *others)

    return apply
```

```python
import functools
import math

import jax
import jax.numpy as jnp
import numpy as np
from jax import lax
from jax.experimental import pallas as pl
from jax.experimental.pallas import tpu as pltpu
from jax.sharding import PartitionSpec as P

D = 8192


def from_behind(value, axis, steps):
    count = lax.axis_size(axis)
    first, last = (max(0, -steps), min(count, count - steps))
    return lax.ppermute(value, axis, [(source, source + steps) for source in range(first, last)])


def rotation(first_index, second_index, period):
    product = first_index[:, None] * second_index[None, :] % period
    angle = product.astype(jnp.float32) * (2.0 * math.pi / period)
    return (jnp.cos(angle), jnp.sin(angle))


def halves(values):
    upper = values.astype(jnp.bfloat16)
    lower = (values - upper.astype(jnp.float32)).astype(jnp.bfloat16)
    return (upper, lower)


def mixing(table, operand, form):
    table_high, table_low = halves(table)
    if operand.dtype == jnp.bfloat16:
        pairs = [(table_high, operand), (table_low, operand)]
    else:
        operand_high, operand_low = halves(operand)
        pairs = [(table_high, operand_high), (table_low, operand_high), (table_high, operand_low)]
    total = None
    for left, right in pairs:
        term = jnp.einsum(form, left, right, preferred_element_type=jnp.float32)
        total = term if total is None else total + term
    return total


def swapped_convolution(gated, long_filter):
    block_rows, local_width = gated.shape
    seq_count = lax.axis_size("seq")
    full_length = 2 * seq_count * block_rows
    signal_in, filter_in = (
        lax.all_to_all(gated[:, None, :], "seq", split_axis=2, concat_axis=1, tiled=True),
        lax.all_to_all(long_filter[:, None, :], "seq", split_axis=2, concat_axis=1, tiled=True),
    )
    freq_short = jnp.arange(2 * seq_count, dtype=jnp.int32)
    cos_short, sin_short = rotation(
        freq_short, jnp.arange(seq_count, dtype=jnp.int32), 2 * seq_count
    )
    long_index = jnp.arange(block_rows, dtype=jnp.int32)
    cos_turn, sin_turn = rotation(long_index, freq_short, full_length)
    cos_turn = cos_turn[:, :, None]
    sin_turn = sin_turn[:, :, None]
    cos_long, sin_long = rotation(long_index, long_index, block_rows)

    def transform(signal):
        real_part = mixing(cos_short, signal, "km,jmc->jkc")
        imag_part = -mixing(sin_short, signal, "km,jmc->jkc")
        twisted_real = (real_part * cos_turn + imag_part * sin_turn).reshape(block_rows, -1)
        twisted_imag = (imag_part * cos_turn - real_part * sin_turn).reshape(block_rows, -1)
        out_real = mixing(cos_long, twisted_real, "kj,jc->kc") + mixing(
            sin_long, twisted_imag, "kj,jc->kc"
        )
        out_imag = mixing(cos_long, twisted_imag, "kj,jc->kc") - mixing(
            sin_long, twisted_real, "kj,jc->kc"
        )
        return (out_real, out_imag)

    signal_real, signal_imag = transform(signal_in)
    filter_real, filter_imag = transform(filter_in)
    prod_real = signal_real * filter_real - signal_imag * filter_imag
    prod_imag = signal_real * filter_imag + signal_imag * filter_real
    back_real = mixing(cos_long, prod_real, "kj,jc->kc") - mixing(sin_long, prod_imag, "kj,jc->kc")
    back_imag = mixing(sin_long, prod_real, "kj,jc->kc") + mixing(cos_long, prod_imag, "kj,jc->kc")
    back_real = back_real.reshape(block_rows, 2 * seq_count, -1)
    back_imag = back_imag.reshape(block_rows, 2 * seq_count, -1)
    turned_real = back_real * cos_turn - back_imag * sin_turn
    turned_imag = back_real * sin_turn + back_imag * cos_turn
    result = (
        mixing(cos_short.T, turned_real, "mk,jkc->jmc")
        - mixing(sin_short.T, turned_imag, "mk,jkc->jmc")
    ) / full_length
    gathered = lax.all_to_all(result, "seq", split_axis=1, concat_axis=2, tiled=True)
    return gathered.reshape(block_rows, local_width)


def shards(
    query_stream, key_stream, value_stream, short_filters, long_filter, skip_bias, norm_gain
):
    block_rows = query_stream.shape[0]
    tap_count = short_filters.shape[1]
    stacked = jnp.stack([query_stream, key_stream, value_stream])
    previous = from_behind(stacked[:, block_rows - tap_count + 1 :, :], "seq", 1)
    extended = jnp.concatenate([previous, stacked], axis=1).astype(jnp.float32)
    convolved = jnp.zeros(stacked.shape, jnp.float32)
    for offset in range(tap_count):
        start = tap_count - 1 - offset
        convolved = (
            convolved
            + short_filters[:, offset, None, :] * extended[:, start : start + block_rows, :]
        )
    query_conv = convolved[0]
    gated = (convolved[1] * convolved[2]).astype(jnp.bfloat16)
    long_out = swapped_convolution(gated, long_filter)
    mixed = jax.nn.silu(query_conv * (long_out + skip_bias[None, :] * gated.astype(jnp.float32)))
    row_power = lax.psum(jnp.sum(mixed * mixed, axis=1), "chan")
    return mixed * lax.rsqrt(row_power / D + 1e-06)[:, None] * norm_gain[None, :]


MESH = pl.DeviceIdType.MESH
PACK = 16
LANES = 128
SUB = 8
VMEM_BYTES = 60 * 1024 * 1024


def tables(tokens, parts):
    freq = 2 * np.arange(tokens, dtype=np.int64) + 1
    time = np.arange(tokens, dtype=np.int64)
    angle = (freq[:, None] * time[None, :] % (4 * tokens)) * (2.0 * np.pi / (4 * tokens))
    forward = np.concatenate([np.cos(angle), -np.sin(angle)], axis=0)
    backward = forward.T / tokens
    rows = tokens // parts
    backward = backward.reshape(parts, rows, 2 * tokens)
    return (forward.astype(jnp.bfloat16), backward.astype(jnp.bfloat16))


def kernel(
    parts,
    groups,
    query,
    key,
    value,
    taps_in,
    filt,
    skip_in,
    forward_in,
    backward_in,
    mixed,
    power_out,
    extended,
    wide,
    turned,
    taps,
    skip,
    forward,
    backward,
    filter_all,
    gated,
    gated_all,
    query_conv,
    filter_spectrum,
    product,
    result,
    result_all,
    partial,
    power,
    power_all,
    load_sem,
    halo_send,
    halo_recv,
    filter_send,
    filter_recv,
    gated_send,
    gated_recv,
    result_send,
    result_recv,
    power_send,
    power_recv,
):
    me = lax.axis_index("seq")
    group = lax.axis_index("chan")
    rows, width = mixed.shape
    part = width // parts
    tokens = rows * parts
    tap_count = taps.shape[1]

    def columns(owner):
        return pl.ds(pl.multiple_of(owner * part, LANES), part)

    def peer(distance):
        return lax.rem(me + distance, parts)

    def source(distance):
        return lax.rem(me + parts - distance, parts)

    streams = (key, value, query)
    loads = []
    for index, (src, dst) in enumerate(
        (
            (key, extended.at[0, pl.ds(PACK, rows), :]),
            (value, extended.at[1, pl.ds(PACK, rows), :]),
            (taps_in, taps),
            (query, extended.at[2, pl.ds(PACK, rows), :]),
            (filt.at[:, columns(me)], filter_all.at[me]),
            (forward_in, forward),
            (skip_in, skip),
            (backward_in, backward),
        )
    ):
        copy = pltpu.make_async_copy(src, dst, load_sem.at[index])
        copy.start()
        loads.append(copy)

    barrier = pltpu.get_barrier_semaphore()
    for distance in range(1, parts):
        pl.semaphore_signal(
            barrier, inc=1, device_id={"seq": peer(distance)}, device_id_type=MESH
        )
    for distance in range(1, groups):
        pl.semaphore_signal(
            barrier,
            inc=1,
            device_id={"chan": lax.rem(group + distance, groups)},
            device_id_type=MESH,
        )
    pl.semaphore_wait(barrier, parts + groups - 2)

    halos = []
    for index in range(3):
        copy = pltpu.make_async_remote_copy(
            src_ref=streams[index].at[pl.ds(rows - PACK, PACK), :],
            dst_ref=extended.at[index, pl.ds(0, PACK), :],
            send_sem=halo_send.at[index],
            recv_sem=halo_recv.at[index],
            device_id={"seq": peer(1)},
            device_id_type=MESH,
        )
        copy.start()
        halos.append(copy)

    def exchange(src, dst, send_sem, recv_sem, distance):
        copy = pltpu.make_async_remote_copy(
            src_ref=src,
            dst_ref=dst.at[me],
            send_sem=send_sem.at[distance - 1],
            recv_sem=recv_sem.at[distance - 1],
            device_id={"seq": peer(distance)},
            device_id_type=MESH,
        )
        copy.start()
        return copy

    filter_copies = [
        exchange(filt.at[:, columns(peer(d))], filter_all, filter_send, filter_recv, d)
        for d in range(1, parts)
    ]

    def ready(index):
        halos[index].wait_recv()

        @pl.when(me == 0)
        def _():
            extended[index, pl.ds(0, PACK), :] = jnp.zeros((PACK, width), extended.dtype)

    block = 64
    tiles = part // LANES
    lane_tiles = width // LANES
    run = rows // SUB

    def lanes_of(tile_at):
        return pl.ds(pl.multiple_of(tile_at * LANES, LANES), LANES)

    def widen(index):
        def body(tile_at, _):
            wide[index, tile_at, pl.ds(SUB, rows), :] = extended[
                index, pl.ds(PACK, rows), lanes_of(tile_at)
            ].astype(jnp.float32)
            return 0

        lax.fori_loop(0, lane_tiles, body, 0)

    def widen_halo(index):
        def body(tile_at, _):
            wide[index, tile_at, pl.ds(0, SUB), :] = extended[
                index, pl.ds(0, PACK), lanes_of(tile_at)
            ].astype(jnp.float32)[PACK - SUB :]
            return 0

        lax.fori_loop(0, lane_tiles, body, 0)

    def short(index, weight, tile_at):
        held = {
            at: wide[index, tile_at, pl.ds(SUB + at, SUB, stride=run), :]
            for at in range(1 - tap_count, run)
        }
        scale = [taps[weight, pl.ds(i, 1), lanes_of(tile_at)] for i in range(tap_count)]
        for at in range(run):
            total = scale[0] * held[at]
            for i in range(1, tap_count):
                total = total + scale[i] * held[at - i]
            yield at, total

    def gate(owner, group_at):
        tile_at = owner * tiles + group_at
        for (at, first), (_, second) in zip(short(0, 1, tile_at), short(1, 2, tile_at)):
            turned[pl.ds(at, SUB, stride=run), :] = first * second
        gated[owner, group_at] = turned[...].astype(gated.dtype)

    for index in range(3):
        loads[index].wait()
    widen(0)
    widen(1)
    ready(0)
    widen_halo(0)
    ready(1)
    widen_halo(1)

    gated_copies = [[] for _ in range(tiles)]
    for group_at in range(tiles):
        for d in (*range(1, parts), 0):
            owner = peer(d)
            gate(owner, group_at)
            if d:
                gated_copies[group_at].append(
                    exchange(
                        gated.at[owner, group_at],
                        gated_all.at[group_at],
                        gated_send.at[group_at],
                        gated_recv.at[group_at],
                        d,
                    )
                )
        gated_all[group_at, me] = gated[me, group_at]

    loads[3].wait()
    widen(2)
    ready(2)
    widen_halo(2)

    def query_step(tile_at, _):
        for at, total in short(2, 0, tile_at):
            query_conv[tile_at, pl.ds(at, SUB, stride=run), :] = total
        return 0

    lax.fori_loop(0, lane_tiles, query_step, 0)

    loads[4].wait()
    loads[5].wait()
    for copy in filter_copies:
        copy.wait_recv()
    tile = 256

    def transform(first, held):
        return jnp.dot(
            forward[pl.ds(first, tile), :],
            held[...].reshape(tokens, -1),
            preferred_element_type=jnp.float32,
        )

    for first in range(0, 2 * tokens, tile):
        filter_spectrum[pl.ds(first, tile), :] = transform(first, filter_all)

    result_copies = [[] for _ in range(tiles)]
    for group_at in range(tiles):
        for copy in gated_copies[group_at]:
            copy.wait_recv()
        lanes = pl.ds(group_at * LANES, LANES)
        held = gated_all.at[group_at]
        for first in range(0, tokens, tile):
            real, imag = pl.ds(first, tile), pl.ds(tokens + first, tile)
            a, b = transform(first, held), transform(tokens + first, held)
            c, d = filter_spectrum[real, lanes], filter_spectrum[imag, lanes]
            product[group_at, real, :] = (a * c - b * d).astype(product.dtype)
            product[group_at, imag, :] = (a * d + b * c).astype(product.dtype)
        if group_at == 0:
            loads[7].wait()
        for d in (*range(1, parts), 0):
            owner = peer(d)
            result[group_at, owner] = jnp.dot(
                backward[owner], product[group_at], preferred_element_type=jnp.float32
            ).astype(result.dtype)
            if d:
                result_copies[group_at].append(
                    exchange(
                        result.at[group_at, owner],
                        result_all.at[group_at],
                        result_send.at[group_at],
                        result_recv.at[group_at],
                        d,
                    )
                )

    loads[6].wait()
    partial[...] = jnp.zeros_like(partial)

    def finish(owner, group_at, held):
        tile_at = owner * tiles + group_at
        lanes = lanes_of(tile_at)

        def step_body(step, _):
            at = pl.ds(pl.multiple_of(step * block, block), block)
            long_out = held[group_at, owner, at, :].astype(jnp.float32)
            direct = skip[:, lanes] * gated[owner, group_at, at, :].astype(jnp.float32)
            x = query_conv[tile_at, at, :] * (long_out + direct)
            y = x / (1.0 + jnp.exp(-x))
            mixed[at, lanes] = y
            partial[at, :] = partial[at, :] + y * y
            return 0

        lax.fori_loop(0, rows // block, step_body, 0)

    for group_at in range(tiles):
        finish(me, group_at, result)
        for d in range(1, parts):
            result_copies[group_at][d - 1].wait_recv()
            finish(source(d), group_at, result_all)

    power[...] = jnp.broadcast_to(
        jnp.sum(partial[...].T, axis=0, keepdims=True), power.shape
    )
    power_copies = []
    for distance in range(1, groups):
        copy = pltpu.make_async_remote_copy(
            src_ref=power,
            dst_ref=power_all.at[group],
            send_sem=power_send.at[distance - 1],
            recv_sem=power_recv.at[distance - 1],
            device_id={"chan": lax.rem(group + distance, groups)},
            device_id_type=MESH,
        )
        copy.start()
        power_copies.append(copy)
    power_all[group] = power[...]
    for copy in (*halos, *filter_copies, *sum(gated_copies + result_copies, [])):
        copy.wait_send()
    for copy in power_copies:
        copy.wait()
    power_out[...] = jnp.sum(power_all[...], axis=0)


SLICES = 8


def normalize(channels, mixed, power, gain, out, scaled, scale, store_sem):
    rows, width = mixed.shape
    count = rows // SLICES
    row_scale = lax.rsqrt(power[pl.ds(0, 1), :] / channels + 1e-06)
    scale[...] = jnp.broadcast_to(row_scale, (LANES, rows)).T
    stores = []
    for index in range(SLICES):
        at = pl.ds(index * count, count)
        factor = scale[at, :]
        for start in range(0, width, LANES):
            lanes = pl.ds(start, LANES)
            scaled[at, lanes] = mixed[at, lanes] * factor * gain[:, lanes]
        copy = pltpu.make_async_copy(scaled.at[at, :], out.at[at, :], store_sem.at[index])
        copy.start()
        stores.append(copy)
    for copy in stores:
        copy.wait()


def fused(
    query_stream, key_stream, value_stream, short_filters, long_filter, skip_bias, norm_gain
):
    rows, width = query_stream.shape
    parts = lax.axis_size("seq")
    groups = lax.axis_size("chan")
    tokens = rows * parts
    part = width // parts
    tiles = part // LANES
    forward, backward = tables(tokens, parts)
    dma = pltpu.SemaphoreType.DMA
    bf16, f32 = jnp.bfloat16, jnp.float32
    mixed, power = pl.pallas_call(
        functools.partial(kernel, parts, groups),
        out_shape=(pltpu.VMEM((rows, width), f32), pltpu.VMEM((8, rows), f32)),
        in_specs=[pl.BlockSpec(memory_space=pl.ANY)] * 8,
        out_specs=(
            pl.BlockSpec(memory_space=pltpu.VMEM),
            pl.BlockSpec(memory_space=pltpu.VMEM),
        ),
        scratch_shapes=[
            pltpu.VMEM((3, rows + PACK, width), bf16),
            pltpu.VMEM((3, width // LANES, rows + SUB, LANES), f32),
            pltpu.VMEM((rows, LANES), f32),
            pltpu.VMEM(short_filters.shape, f32),
            pltpu.VMEM((1, width), f32),
            pltpu.VMEM(forward.shape, bf16),
            pltpu.VMEM(backward.shape, bf16),
            pltpu.VMEM((parts, rows, part), bf16),
            pltpu.VMEM((parts, tiles, rows, LANES), bf16),
            pltpu.VMEM((tiles, parts, rows, LANES), bf16),
            pltpu.VMEM((width // LANES, rows, LANES), f32),
            pltpu.VMEM((2 * tokens, part), f32),
            pltpu.VMEM((tiles, 2 * tokens, LANES), bf16),
            pltpu.VMEM((tiles, parts, rows, LANES), bf16),
            pltpu.VMEM((tiles, parts, rows, LANES), bf16),
            pltpu.VMEM((rows, LANES), f32),
            pltpu.VMEM((8, rows), f32),
            pltpu.VMEM((groups, 8, rows), f32),
            dma((8,)),
            dma((3,)),
            dma((3,)),
            dma((parts - 1,)),
            dma((parts - 1,)),
            dma((tiles, parts - 1)),
            dma((tiles, parts - 1)),
            dma((tiles, parts - 1)),
            dma((tiles, parts - 1)),
            dma((groups - 1,)),
            dma((groups - 1,)),
        ],
        compiler_params=pltpu.CompilerParams(
            collective_id=0, has_side_effects=True, vmem_limit_bytes=VMEM_BYTES
        ),
    )(
        query_stream,
        key_stream,
        value_stream,
        short_filters,
        long_filter,
        skip_bias[None, :],
        jnp.asarray(forward),
        jnp.asarray(backward),
    )
    return pl.pallas_call(
        functools.partial(normalize, width * groups),
        out_shape=jax.ShapeDtypeStruct((rows, width), f32),
        in_specs=[pl.BlockSpec(memory_space=pltpu.VMEM)] * 3,
        out_specs=pl.BlockSpec(memory_space=pl.ANY),
        scratch_shapes=[
            pltpu.VMEM((rows, width), f32),
            pltpu.VMEM((rows, LANES), f32),
            dma((SLICES,)),
        ],
        compiler_params=pltpu.CompilerParams(vmem_limit_bytes=16 * 1024 * 1024),
    )(mixed, power, norm_gain[None, :])


def dense_fits(mesh, shape):
    tokens, channels = shape
    part = channels // (mesh.shape["chan"] * mesh.shape["seq"])
    rows = tokens // mesh.shape["seq"]
    return (
        part % LANES == 0
        and rows % 256 == 0
        and mesh.shape["seq"] > 1
        and mesh.shape["chan"] > 1
        and 8 * tokens * tokens <= VMEM_BYTES // 4
    )


def solution(mesh):
    placed = (
        P("seq", "chan"),
        P("seq", "chan"),
        P("seq", "chan"),
        P(None, None, "chan"),
        P("seq", "chan"),
        P("chan"),
        P("chan"),
    )

    def apply(query_stream, *others):
        body = fused if dense_fits(mesh, query_stream.shape) else shards
        return jax.shard_map(
            body, mesh=mesh, in_specs=placed, out_specs=P("seq", "chan"), check_vma=False
        )(query_stream, *others)

    return apply
```

```python
import functools
import math

import jax
import jax.numpy as jnp
import numpy as np
from jax import lax
from jax.experimental import pallas as pl
from jax.experimental.pallas import tpu as pltpu
from jax.sharding import PartitionSpec as P

D = 8192


def from_behind(value, axis, steps):
    count = lax.axis_size(axis)
    first, last = (max(0, -steps), min(count, count - steps))
    return lax.ppermute(value, axis, [(source, source + steps) for source in range(first, last)])


def rotation(first_index, second_index, period):
    product = first_index[:, None] * second_index[None, :] % period
    angle = product.astype(jnp.float32) * (2.0 * math.pi / period)
    return (jnp.cos(angle), jnp.sin(angle))


def halves(values):
    upper = values.astype(jnp.bfloat16)
    lower = (values - upper.astype(jnp.float32)).astype(jnp.bfloat16)
    return (upper, lower)


def mixing(table, operand, form):
    table_high, table_low = halves(table)
    if operand.dtype == jnp.bfloat16:
        pairs = [(table_high, operand), (table_low, operand)]
    else:
        operand_high, operand_low = halves(operand)
        pairs = [(table_high, operand_high), (table_low, operand_high), (table_high, operand_low)]
    total = None
    for left, right in pairs:
        term = jnp.einsum(form, left, right, preferred_element_type=jnp.float32)
        total = term if total is None else total + term
    return total


def swapped_convolution(gated, long_filter):
    block_rows, local_width = gated.shape
    seq_count = lax.axis_size("seq")
    full_length = 2 * seq_count * block_rows
    signal_in, filter_in = (
        lax.all_to_all(gated[:, None, :], "seq", split_axis=2, concat_axis=1, tiled=True),
        lax.all_to_all(long_filter[:, None, :], "seq", split_axis=2, concat_axis=1, tiled=True),
    )
    freq_short = jnp.arange(2 * seq_count, dtype=jnp.int32)
    cos_short, sin_short = rotation(
        freq_short, jnp.arange(seq_count, dtype=jnp.int32), 2 * seq_count
    )
    long_index = jnp.arange(block_rows, dtype=jnp.int32)
    cos_turn, sin_turn = rotation(long_index, freq_short, full_length)
    cos_turn = cos_turn[:, :, None]
    sin_turn = sin_turn[:, :, None]
    cos_long, sin_long = rotation(long_index, long_index, block_rows)

    def transform(signal):
        real_part = mixing(cos_short, signal, "km,jmc->jkc")
        imag_part = -mixing(sin_short, signal, "km,jmc->jkc")
        twisted_real = (real_part * cos_turn + imag_part * sin_turn).reshape(block_rows, -1)
        twisted_imag = (imag_part * cos_turn - real_part * sin_turn).reshape(block_rows, -1)
        out_real = mixing(cos_long, twisted_real, "kj,jc->kc") + mixing(
            sin_long, twisted_imag, "kj,jc->kc"
        )
        out_imag = mixing(cos_long, twisted_imag, "kj,jc->kc") - mixing(
            sin_long, twisted_real, "kj,jc->kc"
        )
        return (out_real, out_imag)

    signal_real, signal_imag = transform(signal_in)
    filter_real, filter_imag = transform(filter_in)
    prod_real = signal_real * filter_real - signal_imag * filter_imag
    prod_imag = signal_real * filter_imag + signal_imag * filter_real
    back_real = mixing(cos_long, prod_real, "kj,jc->kc") - mixing(sin_long, prod_imag, "kj,jc->kc")
    back_imag = mixing(sin_long, prod_real, "kj,jc->kc") + mixing(cos_long, prod_imag, "kj,jc->kc")
    back_real = back_real.reshape(block_rows, 2 * seq_count, -1)
    back_imag = back_imag.reshape(block_rows, 2 * seq_count, -1)
    turned_real = back_real * cos_turn - back_imag * sin_turn
    turned_imag = back_real * sin_turn + back_imag * cos_turn
    result = (
        mixing(cos_short.T, turned_real, "mk,jkc->jmc")
        - mixing(sin_short.T, turned_imag, "mk,jkc->jmc")
    ) / full_length
    gathered = lax.all_to_all(result, "seq", split_axis=1, concat_axis=2, tiled=True)
    return gathered.reshape(block_rows, local_width)


def shards(
    query_stream, key_stream, value_stream, short_filters, long_filter, skip_bias, norm_gain
):
    block_rows = query_stream.shape[0]
    tap_count = short_filters.shape[1]
    stacked = jnp.stack([query_stream, key_stream, value_stream])
    previous = from_behind(stacked[:, block_rows - tap_count + 1 :, :], "seq", 1)
    extended = jnp.concatenate([previous, stacked], axis=1).astype(jnp.float32)
    convolved = jnp.zeros(stacked.shape, jnp.float32)
    for offset in range(tap_count):
        start = tap_count - 1 - offset
        convolved = (
            convolved
            + short_filters[:, offset, None, :] * extended[:, start : start + block_rows, :]
        )
    query_conv = convolved[0]
    gated = (convolved[1] * convolved[2]).astype(jnp.bfloat16)
    long_out = swapped_convolution(gated, long_filter)
    mixed = jax.nn.silu(query_conv * (long_out + skip_bias[None, :] * gated.astype(jnp.float32)))
    row_power = lax.psum(jnp.sum(mixed * mixed, axis=1), "chan")
    return mixed * lax.rsqrt(row_power / D + 1e-06)[:, None] * norm_gain[None, :]


MESH = pl.DeviceIdType.MESH
PACK = 16
LANES = 128
SUB = 8
SQUARE = 4
VMEM_BYTES = 60 * 1024 * 1024


def tables(tokens, parts):
    freq = 2 * np.arange(tokens, dtype=np.int64) + 1
    time = np.arange(tokens, dtype=np.int64)
    angle = (freq[:, None] * time[None, :] % (4 * tokens)) * (2.0 * np.pi / (4 * tokens))
    forward = np.concatenate([np.cos(angle), -np.sin(angle)], axis=0)
    backward = forward.T / tokens
    rows = tokens // parts
    backward = backward.reshape(parts, rows, 2 * tokens)
    return (forward.astype(jnp.bfloat16), backward.astype(jnp.bfloat16))


def kernel(
    parts,
    groups,
    query,
    key,
    value,
    taps_in,
    filt,
    skip_in,
    forward_in,
    backward_in,
    mixed,
    power_out,
    extended,
    wide,
    turned,
    taps,
    skip,
    forward,
    backward,
    filter_all,
    gated,
    gated_all,
    query_conv,
    filter_spectrum,
    product,
    result,
    result_all,
    relays,
    partial,
    power,
    power_all,
    load_sem,
    halo_send,
    halo_recv,
    swap_send,
    swap_recv,
    power_send,
    power_recv,
):
    me = lax.axis_index("seq")
    group = lax.axis_index("chan")
    rows, width = mixed.shape
    part = width // parts
    tokens = rows * parts
    tap_count = taps.shape[1]

    def columns(owner):
        return pl.ds(pl.multiple_of(owner * part, LANES), part)

    def peer(distance):
        return lax.rem(me + distance, parts)

    streams = (key, value, query)
    loads = []
    for index, (src, dst) in enumerate(
        (
            (key, extended.at[0, pl.ds(PACK, rows), :]),
            (value, extended.at[1, pl.ds(PACK, rows), :]),
            (taps_in, taps),
            (query, extended.at[2, pl.ds(PACK, rows), :]),
            (filt.at[:, columns(me)], filter_all.at[me]),
            (forward_in, forward),
            (skip_in, skip),
            (backward_in, backward),
        )
    ):
        copy = pltpu.make_async_copy(src, dst, load_sem.at[index])
        copy.start()
        loads.append(copy)

    barrier = pltpu.get_barrier_semaphore()
    for distance in range(1, parts):
        pl.semaphore_signal(
            barrier, inc=1, device_id={"seq": peer(distance)}, device_id_type=MESH
        )
    for distance in range(1, groups):
        pl.semaphore_signal(
            barrier,
            inc=1,
            device_id={"chan": lax.rem(group + distance, groups)},
            device_id_type=MESH,
        )
    pl.semaphore_wait(barrier, parts + groups - 2)

    halos = []
    for index in range(3):
        copy = pltpu.make_async_remote_copy(
            src_ref=streams[index].at[pl.ds(rows - PACK, PACK), :],
            dst_ref=extended.at[index, pl.ds(0, PACK), :],
            send_sem=halo_send.at[index],
            recv_sem=halo_recv.at[index],
            device_id={"seq": peer(1)},
            device_id_type=MESH,
        )
        copy.start()
        halos.append(copy)

    along = me + 1 - 2 * lax.rem(me, 2)
    across = lax.rem(me + 2, parts)
    far = parts - 1 - me

    def route(group_at):
        return (along, across) if group_at % 2 == 0 else (across, along)

    class Exchange:
        def __init__(self, kind, group_at, block, place):
            self.kind, self.group_at = kind, group_at
            self.block, self.place = block, place
            self.via, self.other = route(group_at)
            self.copies = []

        def remote(self, index, src, dst, target):
            copy = pltpu.make_async_remote_copy(
                src_ref=src,
                dst_ref=dst,
                send_sem=swap_send.at[self.kind, self.group_at, index],
                recv_sem=swap_recv.at[self.kind, self.group_at, index],
                device_id={"seq": target},
                device_id_type=MESH,
            )
            copy.start()
            self.copies.append(copy)

        def relay(self):
            return relays.at[self.kind, self.group_at]

        def send_far(self):
            self.remote(0, self.block(far), self.relay(), self.via)

        def send_via(self):
            self.remote(1, self.block(self.via), self.place(me), self.via)

        def send_other(self):
            self.remote(2, self.block(self.other), self.place(me), self.other)

        def forward(self):
            self.copies[0].wait_recv()
            self.remote(3, self.relay(), self.place(self.via), self.other)

        def steps(self):
            return (
                (far, self.send_far),
                (self.via, self.send_via),
                (self.other, self.send_other),
            )

        def arrivals(self):
            return ((self.via, 1), (self.other, 2), (far, 3))

    part_tiles = part // LANES

    def filter_exchange(group_at):
        inner = pl.ds(group_at * LANES, LANES)

        def block(owner):
            at = pl.multiple_of(owner * part + group_at * LANES, LANES)
            return filt.at[:, pl.ds(at, LANES)]

        return Exchange(0, group_at, block, lambda slot: filter_all.at[slot, :, inner])

    filter_swaps = [filter_exchange(group_at) for group_at in range(part_tiles)]
    for swap in filter_swaps:
        swap.send_far()
    for swap in filter_swaps:
        swap.send_via()
        swap.send_other()

    def ready(index):
        halos[index].wait_recv()

        @pl.when(me == 0)
        def _():
            extended[index, pl.ds(0, PACK), :] = jnp.zeros((PACK, width), extended.dtype)

    block = 64
    tiles = part // LANES
    lane_tiles = width // LANES
    run = rows // SUB

    def lanes_of(tile_at):
        return pl.ds(pl.multiple_of(tile_at * LANES, LANES), LANES)

    def widen(index):
        def body(tile_at, _):
            wide[index, tile_at, pl.ds(SUB, rows), :] = extended[
                index, pl.ds(PACK, rows), lanes_of(tile_at)
            ].astype(jnp.float32)
            return 0

        lax.fori_loop(0, lane_tiles, body, 0)

    def widen_halo(index):
        def body(tile_at, _):
            wide[index, tile_at, pl.ds(0, SUB), :] = extended[
                index, pl.ds(0, PACK), lanes_of(tile_at)
            ].astype(jnp.float32)[PACK - SUB :]
            return 0

        lax.fori_loop(0, lane_tiles, body, 0)

    def short(index, weight, tile_at):
        held = {
            at: wide[index, tile_at, pl.ds(SUB + at, SUB, stride=run), :]
            for at in range(1 - tap_count, run)
        }
        scale = [taps[weight, pl.ds(i, 1), lanes_of(tile_at)] for i in range(tap_count)]
        for at in range(run):
            total = scale[0] * held[at]
            for i in range(1, tap_count):
                total = total + scale[i] * held[at - i]
            yield at, total

    def gate(owner, group_at):
        tile_at = owner * tiles + group_at
        for (at, first), (_, second) in zip(short(0, 1, tile_at), short(1, 2, tile_at)):
            turned[pl.ds(at, SUB, stride=run), :] = first * second
        gated[owner, group_at] = turned[...].astype(gated.dtype)

    for index in range(3):
        loads[index].wait()
    widen(0)
    widen(1)
    ready(0)
    widen_halo(0)
    ready(1)
    widen_halo(1)

    gated_swaps = []
    for group_at in range(tiles):
        swap = Exchange(
            1,
            group_at,
            lambda owner, group_at=group_at: gated.at[owner, group_at],
            lambda slot, group_at=group_at: gated_all.at[group_at, slot],
        )
        gated_swaps.append(swap)
        for owner, send in swap.steps():
            gate(owner, group_at)
            send()
        gate(me, group_at)
        gated_all[group_at, me] = gated[me, group_at]
        if group_at == 0:
            for earlier in filter_swaps:
                earlier.forward()

    loads[3].wait()
    widen(2)
    ready(2)
    widen_halo(2)

    def query_step(tile_at, _):
        for at, total in short(2, 0, tile_at):
            query_conv[tile_at, pl.ds(at, SUB, stride=run), :] = total
        return 0

    lax.fori_loop(0, lane_tiles, query_step, 0)

    loads[4].wait()
    loads[5].wait()
    for swap in filter_swaps:
        for _, index in swap.arrivals():
            swap.copies[index].wait_recv()
    tile = 256

    def transform(first, held):
        return jnp.dot(
            forward[pl.ds(first, tile), :],
            held[...].reshape(tokens, -1),
            preferred_element_type=jnp.float32,
        )

    for first in range(0, 2 * tokens, tile):
        if first == tokens:
            gated_swaps[0].forward()
        filter_spectrum[pl.ds(first, tile), :] = transform(first, filter_all)

    result_swaps = []
    for group_at in range(tiles):
        for _, index in gated_swaps[group_at].arrivals():
            gated_swaps[group_at].copies[index].wait_recv()
        lanes = pl.ds(group_at * LANES, LANES)
        held = gated_all.at[group_at]
        for first in range(0, tokens, tile):
            real, imag = pl.ds(first, tile), pl.ds(tokens + first, tile)
            a, b = transform(first, held), transform(tokens + first, held)
            c, d = filter_spectrum[real, lanes], filter_spectrum[imag, lanes]
            product[group_at, real, :] = (a * c - b * d).astype(product.dtype)
            product[group_at, imag, :] = (a * d + b * c).astype(product.dtype)
        if group_at == 0:
            loads[7].wait()
        if group_at + 1 < tiles:
            gated_swaps[group_at + 1].forward()
        if group_at:
            result_swaps[group_at - 1].forward()

        def back(owner, group_at=group_at):
            result[group_at, owner] = jnp.dot(
                backward[owner], product[group_at], preferred_element_type=jnp.float32
            ).astype(result.dtype)

        swap = Exchange(
            2,
            group_at,
            lambda owner, group_at=group_at: result.at[group_at, owner],
            lambda slot, group_at=group_at: result_all.at[group_at, slot],
        )
        result_swaps.append(swap)
        for owner, send in swap.steps():
            back(owner)
            send()
        back(me)

    loads[6].wait()
    partial[...] = jnp.zeros_like(partial)

    def finish(owner, group_at, held):
        tile_at = owner * tiles + group_at
        lanes = lanes_of(tile_at)

        def step_body(step, _):
            at = pl.ds(pl.multiple_of(step * block, block), block)
            long_out = held[group_at, owner, at, :].astype(jnp.float32)
            direct = skip[:, lanes] * gated[owner, group_at, at, :].astype(jnp.float32)
            x = query_conv[tile_at, at, :] * (long_out + direct)
            y = x / (1.0 + jnp.exp(-x))
            mixed[at, lanes] = y
            partial[at, :] = partial[at, :] + y * y
            return 0

        lax.fori_loop(0, rows // block, step_body, 0)

    for group_at in range(tiles):
        finish(me, group_at, result)
    for group_at in range(tiles):
        swap = result_swaps[group_at]
        for source, index in swap.arrivals():
            if index == 3 and group_at + 1 == tiles - 1:
                result_swaps[group_at + 1].forward()
            if tiles == 1 and index == 3:
                swap.forward()
            swap.copies[index].wait_recv()
            finish(source, group_at, result_all)

    power[...] = jnp.broadcast_to(
        jnp.sum(partial[...].T, axis=0, keepdims=True), power.shape
    )
    power_copies = []
    for distance in range(1, groups):
        copy = pltpu.make_async_remote_copy(
            src_ref=power,
            dst_ref=power_all.at[group],
            send_sem=power_send.at[distance - 1],
            recv_sem=power_recv.at[distance - 1],
            device_id={"chan": lax.rem(group + distance, groups)},
            device_id_type=MESH,
        )
        copy.start()
        power_copies.append(copy)
    power_all[group] = power[...]
    for copy in halos:
        copy.wait_send()
    for swap in (*filter_swaps, *gated_swaps, *result_swaps):
        for copy in swap.copies:
            copy.wait_send()
    for copy in power_copies:
        copy.wait()
    power_out[...] = jnp.sum(power_all[...], axis=0)


SLICES = 8


def normalize(channels, mixed, power, gain, out, scaled, scale, store_sem):
    rows, width = mixed.shape
    count = rows // SLICES
    row_scale = lax.rsqrt(power[pl.ds(0, 1), :] / channels + 1e-06)
    scale[...] = jnp.broadcast_to(row_scale, (LANES, rows)).T
    stores = []
    for index in range(SLICES):
        at = pl.ds(index * count, count)
        factor = scale[at, :]
        for start in range(0, width, LANES):
            lanes = pl.ds(start, LANES)
            scaled[at, lanes] = mixed[at, lanes] * factor * gain[:, lanes]
        copy = pltpu.make_async_copy(scaled.at[at, :], out.at[at, :], store_sem.at[index])
        copy.start()
        stores.append(copy)
    for copy in stores:
        copy.wait()


def fused(
    query_stream, key_stream, value_stream, short_filters, long_filter, skip_bias, norm_gain
):
    rows, width = query_stream.shape
    parts = lax.axis_size("seq")
    groups = lax.axis_size("chan")
    tokens = rows * parts
    part = width // parts
    tiles = part // LANES
    forward, backward = tables(tokens, parts)
    dma = pltpu.SemaphoreType.DMA
    bf16, f32 = jnp.bfloat16, jnp.float32
    mixed, power = pl.pallas_call(
        functools.partial(kernel, parts, groups),
        out_shape=(pltpu.VMEM((rows, width), f32), pltpu.VMEM((8, rows), f32)),
        in_specs=[pl.BlockSpec(memory_space=pl.ANY)] * 8,
        out_specs=(
            pl.BlockSpec(memory_space=pltpu.VMEM),
            pl.BlockSpec(memory_space=pltpu.VMEM),
        ),
        scratch_shapes=[
            pltpu.VMEM((3, rows + PACK, width), bf16),
            pltpu.VMEM((3, width // LANES, rows + SUB, LANES), f32),
            pltpu.VMEM((rows, LANES), f32),
            pltpu.VMEM(short_filters.shape, f32),
            pltpu.VMEM((1, width), f32),
            pltpu.VMEM(forward.shape, bf16),
            pltpu.VMEM(backward.shape, bf16),
            pltpu.VMEM((parts, rows, part), bf16),
            pltpu.VMEM((parts, tiles, rows, LANES), bf16),
            pltpu.VMEM((tiles, parts, rows, LANES), bf16),
            pltpu.VMEM((width // LANES, rows, LANES), f32),
            pltpu.VMEM((2 * tokens, part), f32),
            pltpu.VMEM((tiles, 2 * tokens, LANES), bf16),
            pltpu.VMEM((tiles, parts, rows, LANES), bf16),
            pltpu.VMEM((tiles, parts, rows, LANES), bf16),
            pltpu.VMEM((3, tiles, rows, LANES), bf16),
            pltpu.VMEM((rows, LANES), f32),
            pltpu.VMEM((8, rows), f32),
            pltpu.VMEM((groups, 8, rows), f32),
            dma((8,)),
            dma((3,)),
            dma((3,)),
            dma((3, tiles, parts)),
            dma((3, tiles, parts)),
            dma((groups - 1,)),
            dma((groups - 1,)),
        ],
        compiler_params=pltpu.CompilerParams(
            collective_id=0, has_side_effects=True, vmem_limit_bytes=VMEM_BYTES
        ),
    )(
        query_stream,
        key_stream,
        value_stream,
        short_filters,
        long_filter,
        skip_bias[None, :],
        jnp.asarray(forward),
        jnp.asarray(backward),
    )
    return pl.pallas_call(
        functools.partial(normalize, width * groups),
        out_shape=jax.ShapeDtypeStruct((rows, width), f32),
        in_specs=[pl.BlockSpec(memory_space=pltpu.VMEM)] * 3,
        out_specs=pl.BlockSpec(memory_space=pl.ANY),
        scratch_shapes=[
            pltpu.VMEM((rows, width), f32),
            pltpu.VMEM((rows, LANES), f32),
            dma((SLICES,)),
        ],
        compiler_params=pltpu.CompilerParams(vmem_limit_bytes=16 * 1024 * 1024),
    )(mixed, power, norm_gain[None, :])


def dense_fits(mesh, shape):
    tokens, channels = shape
    part = channels // (mesh.shape["chan"] * mesh.shape["seq"])
    rows = tokens // mesh.shape["seq"]
    return (
        part % LANES == 0
        and rows % 256 == 0
        and mesh.shape["seq"] == SQUARE
        and mesh.shape["chan"] > 1
        and 8 * tokens * tokens <= VMEM_BYTES // 4
    )


def solution(mesh):
    placed = (
        P("seq", "chan"),
        P("seq", "chan"),
        P("seq", "chan"),
        P(None, None, "chan"),
        P("seq", "chan"),
        P("chan"),
        P("chan"),
    )

    def apply(query_stream, *others):
        body = fused if dense_fits(mesh, query_stream.shape) else shards
        return jax.shard_map(
            body, mesh=mesh, in_specs=placed, out_specs=P("seq", "chan"), check_vma=False
        )(query_stream, *others)

    return apply
```

```python
import functools
import math

import jax
import jax.numpy as jnp
import numpy as np
from jax import lax
from jax.experimental import pallas as pl
from jax.experimental.pallas import tpu as pltpu
from jax.sharding import PartitionSpec as P

D = 8192


def from_behind(value, axis, steps):
    count = lax.axis_size(axis)
    first, last = (max(0, -steps), min(count, count - steps))
    return lax.ppermute(value, axis, [(source, source + steps) for source in range(first, last)])


def rotation(first_index, second_index, period):
    product = first_index[:, None] * second_index[None, :] % period
    angle = product.astype(jnp.float32) * (2.0 * math.pi / period)
    return (jnp.cos(angle), jnp.sin(angle))


def halves(values):
    upper = values.astype(jnp.bfloat16)
    lower = (values - upper.astype(jnp.float32)).astype(jnp.bfloat16)
    return (upper, lower)


def mixing(table, operand, form):
    table_high, table_low = halves(table)
    if operand.dtype == jnp.bfloat16:
        pairs = [(table_high, operand), (table_low, operand)]
    else:
        operand_high, operand_low = halves(operand)
        pairs = [(table_high, operand_high), (table_low, operand_high), (table_high, operand_low)]
    total = None
    for left, right in pairs:
        term = jnp.einsum(form, left, right, preferred_element_type=jnp.float32)
        total = term if total is None else total + term
    return total


def swapped_convolution(gated, long_filter):
    block_rows, local_width = gated.shape
    seq_count = lax.axis_size("seq")
    full_length = 2 * seq_count * block_rows
    signal_in, filter_in = (
        lax.all_to_all(gated[:, None, :], "seq", split_axis=2, concat_axis=1, tiled=True),
        lax.all_to_all(long_filter[:, None, :], "seq", split_axis=2, concat_axis=1, tiled=True),
    )
    freq_short = jnp.arange(2 * seq_count, dtype=jnp.int32)
    cos_short, sin_short = rotation(
        freq_short, jnp.arange(seq_count, dtype=jnp.int32), 2 * seq_count
    )
    long_index = jnp.arange(block_rows, dtype=jnp.int32)
    cos_turn, sin_turn = rotation(long_index, freq_short, full_length)
    cos_turn = cos_turn[:, :, None]
    sin_turn = sin_turn[:, :, None]
    cos_long, sin_long = rotation(long_index, long_index, block_rows)

    def transform(signal):
        real_part = mixing(cos_short, signal, "km,jmc->jkc")
        imag_part = -mixing(sin_short, signal, "km,jmc->jkc")
        twisted_real = (real_part * cos_turn + imag_part * sin_turn).reshape(block_rows, -1)
        twisted_imag = (imag_part * cos_turn - real_part * sin_turn).reshape(block_rows, -1)
        out_real = mixing(cos_long, twisted_real, "kj,jc->kc") + mixing(
            sin_long, twisted_imag, "kj,jc->kc"
        )
        out_imag = mixing(cos_long, twisted_imag, "kj,jc->kc") - mixing(
            sin_long, twisted_real, "kj,jc->kc"
        )
        return (out_real, out_imag)

    signal_real, signal_imag = transform(signal_in)
    filter_real, filter_imag = transform(filter_in)
    prod_real = signal_real * filter_real - signal_imag * filter_imag
    prod_imag = signal_real * filter_imag + signal_imag * filter_real
    back_real = mixing(cos_long, prod_real, "kj,jc->kc") - mixing(sin_long, prod_imag, "kj,jc->kc")
    back_imag = mixing(sin_long, prod_real, "kj,jc->kc") + mixing(cos_long, prod_imag, "kj,jc->kc")
    back_real = back_real.reshape(block_rows, 2 * seq_count, -1)
    back_imag = back_imag.reshape(block_rows, 2 * seq_count, -1)
    turned_real = back_real * cos_turn - back_imag * sin_turn
    turned_imag = back_real * sin_turn + back_imag * cos_turn
    result = (
        mixing(cos_short.T, turned_real, "mk,jkc->jmc")
        - mixing(sin_short.T, turned_imag, "mk,jkc->jmc")
    ) / full_length
    gathered = lax.all_to_all(result, "seq", split_axis=1, concat_axis=2, tiled=True)
    return gathered.reshape(block_rows, local_width)


def shards(
    query_stream, key_stream, value_stream, short_filters, long_filter, skip_bias, norm_gain
):
    block_rows = query_stream.shape[0]
    tap_count = short_filters.shape[1]
    stacked = jnp.stack([query_stream, key_stream, value_stream])
    previous = from_behind(stacked[:, block_rows - tap_count + 1 :, :], "seq", 1)
    extended = jnp.concatenate([previous, stacked], axis=1).astype(jnp.float32)
    convolved = jnp.zeros(stacked.shape, jnp.float32)
    for offset in range(tap_count):
        start = tap_count - 1 - offset
        convolved = (
            convolved
            + short_filters[:, offset, None, :] * extended[:, start : start + block_rows, :]
        )
    query_conv = convolved[0]
    gated = (convolved[1] * convolved[2]).astype(jnp.bfloat16)
    long_out = swapped_convolution(gated, long_filter)
    mixed = jax.nn.silu(query_conv * (long_out + skip_bias[None, :] * gated.astype(jnp.float32)))
    row_power = lax.psum(jnp.sum(mixed * mixed, axis=1), "chan")
    return mixed * lax.rsqrt(row_power / D + 1e-06)[:, None] * norm_gain[None, :]


MESH = pl.DeviceIdType.MESH
PACK = 16
LANES = 128
SUB = 8
VMEM_BYTES = 60 * 1024 * 1024


def tables(tokens, parts):
    freq = 2 * np.arange(tokens, dtype=np.int64) + 1
    time = np.arange(tokens, dtype=np.int64)
    angle = (freq[:, None] * time[None, :] % (4 * tokens)) * (2.0 * np.pi / (4 * tokens))
    forward = np.concatenate([np.cos(angle), -np.sin(angle)], axis=0)
    backward = forward.T / tokens
    rows = tokens // parts
    backward = backward.reshape(parts, rows, 2 * tokens)
    return (forward.astype(jnp.bfloat16), backward.astype(jnp.bfloat16))


def kernel(
    parts,
    groups,
    query,
    key,
    value,
    taps_in,
    filt,
    skip_in,
    forward_in,
    backward_in,
    mixed,
    power_out,
    extended,
    wide,
    turned,
    taps,
    skip,
    forward,
    backward,
    filter_all,
    gated,
    gated_all,
    query_conv,
    filter_spectrum,
    product,
    result,
    result_all,
    partial,
    power,
    power_all,
    load_sem,
    halo_send,
    halo_recv,
    filter_send,
    filter_recv,
    gated_send,
    gated_recv,
    result_send,
    result_recv,
    power_send,
    power_recv,
):
    me = lax.axis_index("seq")
    group = lax.axis_index("chan")
    rows, width = mixed.shape
    part = width // parts
    tokens = rows * parts
    tap_count = taps.shape[1]

    def columns(owner):
        return pl.ds(pl.multiple_of(owner * part, LANES), part)

    def peer(distance):
        return lax.rem(me + distance, parts)

    def source(distance):
        return lax.rem(me + parts - distance, parts)

    streams = (key, value, query)
    loads = []
    for index, (src, dst) in enumerate(
        (
            (key, extended.at[0, pl.ds(PACK, rows), :]),
            (value, extended.at[1, pl.ds(PACK, rows), :]),
            (taps_in, taps),
            (query, extended.at[2, pl.ds(PACK, rows), :]),
            (filt.at[:, columns(me)], filter_all.at[me]),
            (forward_in, forward),
            (skip_in, skip),
            (backward_in, backward),
        )
    ):
        copy = pltpu.make_async_copy(src, dst, load_sem.at[index])
        if index < 5:
            copy.start()
        loads.append(copy)

    barrier = pltpu.get_barrier_semaphore()
    for distance in range(1, parts):
        pl.semaphore_signal(
            barrier, inc=1, device_id={"seq": peer(distance)}, device_id_type=MESH
        )
    for distance in range(1, groups):
        pl.semaphore_signal(
            barrier,
            inc=1,
            device_id={"chan": lax.rem(group + distance, groups)},
            device_id_type=MESH,
        )
    pl.semaphore_wait(barrier, parts + groups - 2)

    halos = []
    for index in range(3):
        copy = pltpu.make_async_remote_copy(
            src_ref=streams[index].at[pl.ds(rows - PACK, PACK), :],
            dst_ref=extended.at[index, pl.ds(0, PACK), :],
            send_sem=halo_send.at[index],
            recv_sem=halo_recv.at[index],
            device_id={"seq": peer(1)},
            device_id_type=MESH,
        )
        copy.start()
        halos.append(copy)

    def exchange(src, dst, send_sem, recv_sem, distance):
        copy = pltpu.make_async_remote_copy(
            src_ref=src,
            dst_ref=dst.at[me],
            send_sem=send_sem.at[distance - 1],
            recv_sem=recv_sem.at[distance - 1],
            device_id={"seq": peer(distance)},
            device_id_type=MESH,
        )
        copy.start()
        return copy

    filter_copies = [
        exchange(filt.at[:, columns(peer(d))], filter_all, filter_send, filter_recv, d)
        for d in range(1, parts)
    ]
    for copy in loads[5:]:
        copy.start()

    def ready(index):
        halos[index].wait_recv()

        @pl.when(me == 0)
        def _():
            extended[index, pl.ds(0, PACK), :] = jnp.zeros((PACK, width), extended.dtype)

    block = 128
    tiles = part // LANES
    lane_tiles = width // LANES
    run = rows // SUB

    def lanes_of(tile_at):
        return pl.ds(pl.multiple_of(tile_at * LANES, LANES), LANES)

    def widen(index):
        def body(tile_at, _):
            wide[index, tile_at, pl.ds(SUB, rows), :] = extended[
                index, pl.ds(PACK, rows), lanes_of(tile_at)
            ].astype(jnp.float32)
            return 0

        lax.fori_loop(0, lane_tiles, body, 0)

    def widen_halo(index):
        def body(tile_at, _):
            wide[index, tile_at, pl.ds(0, SUB), :] = extended[
                index, pl.ds(0, PACK), lanes_of(tile_at)
            ].astype(jnp.float32)[PACK - SUB :]
            return 0

        lax.fori_loop(0, lane_tiles, body, 0)

    def short(index, weight, tile_at):
        held = {
            at: wide[index, tile_at, pl.ds(SUB + at, SUB, stride=run), :]
            for at in range(1 - tap_count, run)
        }
        scale = [taps[weight, pl.ds(i, 1), lanes_of(tile_at)] for i in range(tap_count)]
        for at in range(run):
            total = scale[0] * held[at]
            for i in range(1, tap_count):
                total = total + scale[i] * held[at - i]
            yield at, total

    def gate(owner, group_at):
        tile_at = owner * tiles + group_at
        for (at, first), (_, second) in zip(short(0, 1, tile_at), short(1, 2, tile_at)):
            turned[pl.ds(at, SUB, stride=run), :] = first * second
        gated[owner, group_at] = turned[...].astype(gated.dtype)

    for index in range(3):
        loads[index].wait()
    widen(0)
    widen(1)
    ready(0)
    widen_halo(0)
    ready(1)
    widen_halo(1)

    gated_copies = [[] for _ in range(tiles)]
    for group_at in range(tiles):
        for d in (*range(1, parts), 0):
            owner = peer(d)
            gate(owner, group_at)
            if d:
                gated_copies[group_at].append(
                    exchange(
                        gated.at[owner, group_at],
                        gated_all.at[group_at],
                        gated_send.at[group_at],
                        gated_recv.at[group_at],
                        d,
                    )
                )
        gated_all[group_at, me] = gated[me, group_at]

    loads[3].wait()
    widen(2)
    ready(2)
    widen_halo(2)

    def query_step(tile_at, _):
        for at, total in short(2, 0, tile_at):
            query_conv[tile_at, pl.ds(at, SUB, stride=run), :] = total
        return 0

    lax.fori_loop(0, lane_tiles, query_step, 0)

    loads[4].wait()
    loads[5].wait()
    for copy in filter_copies:
        copy.wait_recv()
    tile = 256

    def transform(first, held):
        return jnp.dot(
            forward[pl.ds(first, tile), :],
            held[...].reshape(tokens, -1),
            preferred_element_type=jnp.float32,
        )

    for first in range(0, 2 * tokens, tile):
        filter_spectrum[pl.ds(first, tile), :] = transform(first, filter_all)

    result_copies = [[] for _ in range(tiles)]
    for group_at in range(tiles):
        for copy in gated_copies[group_at]:
            copy.wait_recv()
        lanes = pl.ds(group_at * LANES, LANES)
        held = gated_all.at[group_at]
        for first in range(0, tokens, tile):
            real, imag = pl.ds(first, tile), pl.ds(tokens + first, tile)
            a, b = transform(first, held), transform(tokens + first, held)
            c, d = filter_spectrum[real, lanes], filter_spectrum[imag, lanes]
            product[group_at, real, :] = (a * c - b * d).astype(product.dtype)
            product[group_at, imag, :] = (a * d + b * c).astype(product.dtype)
        if group_at == 0:
            loads[7].wait()
        for d in (*range(1, parts), 0):
            owner = peer(d)
            result[group_at, owner] = jnp.dot(
                backward[owner], product[group_at], preferred_element_type=jnp.float32
            ).astype(result.dtype)
            if d:
                result_copies[group_at].append(
                    exchange(
                        result.at[group_at, owner],
                        result_all.at[group_at],
                        result_send.at[group_at],
                        result_recv.at[group_at],
                        d,
                    )
                )

    loads[6].wait()
    partial[...] = jnp.zeros_like(partial)

    def finish(owner, group_at, held):
        tile_at = owner * tiles + group_at
        lanes = lanes_of(tile_at)

        def step_body(step, _):
            at = pl.ds(pl.multiple_of(step * block, block), block)
            long_out = held[group_at, owner, at, :].astype(jnp.float32)
            direct = skip[:, lanes] * gated[owner, group_at, at, :].astype(jnp.float32)
            x = query_conv[tile_at, at, :] * (long_out + direct)
            y = x / (1.0 + jnp.exp(-x))
            mixed[at, lanes] = y
            partial[at, :] = partial[at, :] + y * y
            return 0

        lax.fori_loop(0, rows // block, step_body, 0)

    for group_at in range(tiles):
        finish(me, group_at, result)
        for d in range(1, parts):
            result_copies[group_at][d - 1].wait_recv()
            finish(source(d), group_at, result_all)

    power[...] = jnp.broadcast_to(
        jnp.sum(partial[...].T, axis=0, keepdims=True), power.shape
    )
    power_copies = []
    for distance in range(1, groups):
        copy = pltpu.make_async_remote_copy(
            src_ref=power,
            dst_ref=power_all.at[group],
            send_sem=power_send.at[distance - 1],
            recv_sem=power_recv.at[distance - 1],
            device_id={"chan": lax.rem(group + distance, groups)},
            device_id_type=MESH,
        )
        copy.start()
        power_copies.append(copy)
    power_all[group] = power[...]
    for copy in (*halos, *filter_copies, *sum(gated_copies + result_copies, [])):
        copy.wait_send()
    for copy in power_copies:
        copy.wait()
    power_out[...] = jnp.sum(power_all[...], axis=0)


SLICES = 8


def normalize(channels, mixed, power, gain, out, scaled, scale, store_sem):
    rows, width = mixed.shape
    count = rows // SLICES
    row_scale = lax.rsqrt(power[pl.ds(0, 1), :] / channels + 1e-06)
    scale[...] = jnp.broadcast_to(row_scale, (LANES, rows)).T
    stores = []
    for index in range(SLICES):
        at = pl.ds(index * count, count)
        factor = scale[at, :]
        for start in range(0, width, LANES):
            lanes = pl.ds(start, LANES)
            scaled[at, lanes] = mixed[at, lanes] * factor * gain[:, lanes]
        copy = pltpu.make_async_copy(scaled.at[at, :], out.at[at, :], store_sem.at[index])
        copy.start()
        stores.append(copy)
    for copy in stores:
        copy.wait()


def fused(
    query_stream, key_stream, value_stream, short_filters, long_filter, skip_bias, norm_gain
):
    rows, width = query_stream.shape
    parts = lax.axis_size("seq")
    groups = lax.axis_size("chan")
    tokens = rows * parts
    part = width // parts
    tiles = part // LANES
    forward, backward = tables(tokens, parts)
    dma = pltpu.SemaphoreType.DMA
    bf16, f32 = jnp.bfloat16, jnp.float32
    mixed, power = pl.pallas_call(
        functools.partial(kernel, parts, groups),
        out_shape=(pltpu.VMEM((rows, width), f32), pltpu.VMEM((8, rows), f32)),
        in_specs=[pl.BlockSpec(memory_space=pl.ANY)] * 8,
        out_specs=(
            pl.BlockSpec(memory_space=pltpu.VMEM),
            pl.BlockSpec(memory_space=pltpu.VMEM),
        ),
        scratch_shapes=[
            pltpu.VMEM((3, rows + PACK, width), bf16),
            pltpu.VMEM((3, width // LANES, rows + SUB, LANES), f32),
            pltpu.VMEM((rows, LANES), f32),
            pltpu.VMEM(short_filters.shape, f32),
            pltpu.VMEM((1, width), f32),
            pltpu.VMEM(forward.shape, bf16),
            pltpu.VMEM(backward.shape, bf16),
            pltpu.VMEM((parts, rows, part), bf16),
            pltpu.VMEM((parts, tiles, rows, LANES), bf16),
            pltpu.VMEM((tiles, parts, rows, LANES), bf16),
            pltpu.VMEM((width // LANES, rows, LANES), f32),
            pltpu.VMEM((2 * tokens, part), f32),
            pltpu.VMEM((tiles, 2 * tokens, LANES), bf16),
            pltpu.VMEM((tiles, parts, rows, LANES), bf16),
            pltpu.VMEM((tiles, parts, rows, LANES), bf16),
            pltpu.VMEM((rows, LANES), f32),
            pltpu.VMEM((8, rows), f32),
            pltpu.VMEM((groups, 8, rows), f32),
            dma((8,)),
            dma((3,)),
            dma((3,)),
            dma((parts - 1,)),
            dma((parts - 1,)),
            dma((tiles, parts - 1)),
            dma((tiles, parts - 1)),
            dma((tiles, parts - 1)),
            dma((tiles, parts - 1)),
            dma((groups - 1,)),
            dma((groups - 1,)),
        ],
        compiler_params=pltpu.CompilerParams(
            collective_id=0, has_side_effects=True, vmem_limit_bytes=VMEM_BYTES
        ),
    )(
        query_stream,
        key_stream,
        value_stream,
        short_filters,
        long_filter,
        skip_bias[None, :],
        jnp.asarray(forward),
        jnp.asarray(backward),
    )
    return pl.pallas_call(
        functools.partial(normalize, width * groups),
        out_shape=jax.ShapeDtypeStruct((rows, width), f32),
        in_specs=[pl.BlockSpec(memory_space=pltpu.VMEM)] * 3,
        out_specs=pl.BlockSpec(memory_space=pl.ANY),
        scratch_shapes=[
            pltpu.VMEM((rows, width), f32),
            pltpu.VMEM((rows, LANES), f32),
            dma((SLICES,)),
        ],
        compiler_params=pltpu.CompilerParams(vmem_limit_bytes=16 * 1024 * 1024),
    )(mixed, power, norm_gain[None, :])


def dense_fits(mesh, shape):
    tokens, channels = shape
    part = channels // (mesh.shape["chan"] * mesh.shape["seq"])
    rows = tokens // mesh.shape["seq"]
    return (
        part % LANES == 0
        and rows % 256 == 0
        and mesh.shape["seq"] > 1
        and mesh.shape["chan"] > 1
        and 8 * tokens * tokens <= VMEM_BYTES // 4
    )


def solution(mesh):
    placed = (
        P("seq", "chan"),
        P("seq", "chan"),
        P("seq", "chan"),
        P(None, None, "chan"),
        P("seq", "chan"),
        P("chan"),
        P("chan"),
    )

    def apply(query_stream, *others):
        body = fused if dense_fits(mesh, query_stream.shape) else shards
        return jax.shard_map(
            body, mesh=mesh, in_specs=placed, out_specs=P("seq", "chan"), check_vma=False
        )(query_stream, *others)

    return apply
```

```python
import functools
import math

import jax
import jax.numpy as jnp
import numpy as np
from jax import lax
from jax.experimental import pallas as pl
from jax.experimental.pallas import tpu as pltpu
from jax.sharding import PartitionSpec as P

D = 8192


def from_behind(value, axis, steps):
    count = lax.axis_size(axis)
    first, last = (max(0, -steps), min(count, count - steps))
    return lax.ppermute(value, axis, [(source, source + steps) for source in range(first, last)])


def rotation(first_index, second_index, period):
    product = first_index[:, None] * second_index[None, :] % period
    angle = product.astype(jnp.float32) * (2.0 * math.pi / period)
    return (jnp.cos(angle), jnp.sin(angle))


def halves(values):
    upper = values.astype(jnp.bfloat16)
    lower = (values - upper.astype(jnp.float32)).astype(jnp.bfloat16)
    return (upper, lower)


def mixing(table, operand, form):
    table_high, table_low = halves(table)
    if operand.dtype == jnp.bfloat16:
        pairs = [(table_high, operand), (table_low, operand)]
    else:
        operand_high, operand_low = halves(operand)
        pairs = [(table_high, operand_high), (table_low, operand_high), (table_high, operand_low)]
    total = None
    for left, right in pairs:
        term = jnp.einsum(form, left, right, preferred_element_type=jnp.float32)
        total = term if total is None else total + term
    return total


def swapped_convolution(gated, long_filter):
    block_rows, local_width = gated.shape
    seq_count = lax.axis_size("seq")
    full_length = 2 * seq_count * block_rows
    signal_in, filter_in = (
        lax.all_to_all(gated[:, None, :], "seq", split_axis=2, concat_axis=1, tiled=True),
        lax.all_to_all(long_filter[:, None, :], "seq", split_axis=2, concat_axis=1, tiled=True),
    )
    freq_short = jnp.arange(2 * seq_count, dtype=jnp.int32)
    cos_short, sin_short = rotation(
        freq_short, jnp.arange(seq_count, dtype=jnp.int32), 2 * seq_count
    )
    long_index = jnp.arange(block_rows, dtype=jnp.int32)
    cos_turn, sin_turn = rotation(long_index, freq_short, full_length)
    cos_turn = cos_turn[:, :, None]
    sin_turn = sin_turn[:, :, None]
    cos_long, sin_long = rotation(long_index, long_index, block_rows)

    def transform(signal):
        real_part = mixing(cos_short, signal, "km,jmc->jkc")
        imag_part = -mixing(sin_short, signal, "km,jmc->jkc")
        twisted_real = (real_part * cos_turn + imag_part * sin_turn).reshape(block_rows, -1)
        twisted_imag = (imag_part * cos_turn - real_part * sin_turn).reshape(block_rows, -1)
        out_real = mixing(cos_long, twisted_real, "kj,jc->kc") + mixing(
            sin_long, twisted_imag, "kj,jc->kc"
        )
        out_imag = mixing(cos_long, twisted_imag, "kj,jc->kc") - mixing(
            sin_long, twisted_real, "kj,jc->kc"
        )
        return (out_real, out_imag)

    signal_real, signal_imag = transform(signal_in)
    filter_real, filter_imag = transform(filter_in)
    prod_real = signal_real * filter_real - signal_imag * filter_imag
    prod_imag = signal_real * filter_imag + signal_imag * filter_real
    back_real = mixing(cos_long, prod_real, "kj,jc->kc") - mixing(sin_long, prod_imag, "kj,jc->kc")
    back_imag = mixing(sin_long, prod_real, "kj,jc->kc") + mixing(cos_long, prod_imag, "kj,jc->kc")
    back_real = back_real.reshape(block_rows, 2 * seq_count, -1)
    back_imag = back_imag.reshape(block_rows, 2 * seq_count, -1)
    turned_real = back_real * cos_turn - back_imag * sin_turn
    turned_imag = back_real * sin_turn + back_imag * cos_turn
    result = (
        mixing(cos_short.T, turned_real, "mk,jkc->jmc")
        - mixing(sin_short.T, turned_imag, "mk,jkc->jmc")
    ) / full_length
    gathered = lax.all_to_all(result, "seq", split_axis=1, concat_axis=2, tiled=True)
    return gathered.reshape(block_rows, local_width)


def shards(
    query_stream, key_stream, value_stream, short_filters, long_filter, skip_bias, norm_gain
):
    block_rows = query_stream.shape[0]
    tap_count = short_filters.shape[1]
    stacked = jnp.stack([query_stream, key_stream, value_stream])
    previous = from_behind(stacked[:, block_rows - tap_count + 1 :, :], "seq", 1)
    extended = jnp.concatenate([previous, stacked], axis=1).astype(jnp.float32)
    convolved = jnp.zeros(stacked.shape, jnp.float32)
    for offset in range(tap_count):
        start = tap_count - 1 - offset
        convolved = (
            convolved
            + short_filters[:, offset, None, :] * extended[:, start : start + block_rows, :]
        )
    query_conv = convolved[0]
    gated = (convolved[1] * convolved[2]).astype(jnp.bfloat16)
    long_out = swapped_convolution(gated, long_filter)
    mixed = jax.nn.silu(query_conv * (long_out + skip_bias[None, :] * gated.astype(jnp.float32)))
    row_power = lax.psum(jnp.sum(mixed * mixed, axis=1), "chan")
    return mixed * lax.rsqrt(row_power / D + 1e-06)[:, None] * norm_gain[None, :]


MESH = pl.DeviceIdType.MESH
PACK = 16
LANES = 128
SUB = 8
VMEM_BYTES = 60 * 1024 * 1024


def tables(tokens, parts):
    freq = 2 * np.arange(tokens, dtype=np.int64) + 1
    time = np.arange(tokens, dtype=np.int64)
    angle = (freq[:, None] * time[None, :] % (4 * tokens)) * (2.0 * np.pi / (4 * tokens))
    forward = np.concatenate([np.cos(angle), -np.sin(angle)], axis=0)
    backward = forward.T / tokens
    rows = tokens // parts
    backward = backward.reshape(parts, rows, 2 * tokens)
    return (forward.astype(jnp.bfloat16), backward.astype(jnp.bfloat16))


def kernel(
    parts,
    groups,
    query,
    key,
    value,
    taps_in,
    filt,
    skip_in,
    forward_in,
    backward_in,
    mixed,
    power_out,
    extended,
    wide,
    turned,
    taps,
    skip,
    forward,
    backward,
    filter_all,
    gated,
    gated_all,
    query_conv,
    filter_spectrum,
    product,
    result,
    result_all,
    partial,
    power,
    power_all,
    load_sem,
    halo_send,
    halo_recv,
    filter_send,
    filter_recv,
    gated_send,
    gated_recv,
    result_send,
    result_recv,
    power_send,
    power_recv,
):
    me = lax.axis_index("seq")
    group = lax.axis_index("chan")
    rows, width = mixed.shape
    part = width // parts
    tokens = rows * parts
    tap_count = taps.shape[1]

    def columns(owner):
        return pl.ds(pl.multiple_of(owner * part, LANES), part)

    def peer(distance):
        return lax.rem(me + distance, parts)

    def source(distance):
        return lax.rem(me + parts - distance, parts)

    streams = (key, value, query)
    loads = []
    for index, (src, dst) in enumerate(
        (
            (key, extended.at[0, pl.ds(PACK, rows), :]),
            (value, extended.at[1, pl.ds(PACK, rows), :]),
            (taps_in, taps),
            (query, extended.at[2, pl.ds(PACK, rows), :]),
            (filt.at[:, columns(me)], filter_all.at[me]),
            (forward_in, forward),
            (skip_in, skip),
            (backward_in, backward),
        )
    ):
        copy = pltpu.make_async_copy(src, dst, load_sem.at[index])
        copy.start()
        loads.append(copy)

    barrier = pltpu.get_barrier_semaphore()
    for distance in range(1, parts):
        pl.semaphore_signal(
            barrier, inc=1, device_id={"seq": peer(distance)}, device_id_type=MESH
        )
    for distance in range(1, groups):
        pl.semaphore_signal(
            barrier,
            inc=1,
            device_id={"chan": lax.rem(group + distance, groups)},
            device_id_type=MESH,
        )
    pl.semaphore_wait(barrier, parts + groups - 2)

    halos = []
    for index in range(3):
        copy = pltpu.make_async_remote_copy(
            src_ref=streams[index].at[pl.ds(rows - PACK, PACK), :],
            dst_ref=extended.at[index, pl.ds(0, PACK), :],
            send_sem=halo_send.at[index],
            recv_sem=halo_recv.at[index],
            device_id={"seq": peer(1)},
            device_id_type=MESH,
        )
        copy.start()
        halos.append(copy)

    def exchange(src, dst, send_sem, recv_sem, distance):
        copy = pltpu.make_async_remote_copy(
            src_ref=src,
            dst_ref=dst.at[me],
            send_sem=send_sem.at[distance - 1],
            recv_sem=recv_sem.at[distance - 1],
            device_id={"seq": peer(distance)},
            device_id_type=MESH,
        )
        copy.start()
        return copy

    filter_copies = [
        exchange(filt.at[:, columns(peer(d))], filter_all, filter_send, filter_recv, d)
        for d in range(1, parts)
    ]

    def ready(index):
        halos[index].wait_recv()

        @pl.when(me == 0)
        def _():
            extended[index, pl.ds(0, PACK), :] = jnp.zeros((PACK, width), extended.dtype)

    block = 64
    tiles = part // LANES
    lane_tiles = width // LANES
    run = rows // SUB

    def lanes_of(tile_at):
        return pl.ds(pl.multiple_of(tile_at * LANES, LANES), LANES)

    def widen(index):
        def body(tile_at, _):
            wide[index, tile_at, pl.ds(SUB, rows), :] = extended[
                index, pl.ds(PACK, rows), lanes_of(tile_at)
            ].astype(jnp.float32)
            return 0

        lax.fori_loop(0, lane_tiles, body, 0)

    def widen_halo(index):
        def body(tile_at, _):
            wide[index, tile_at, pl.ds(0, SUB), :] = extended[
                index, pl.ds(0, PACK), lanes_of(tile_at)
            ].astype(jnp.float32)[PACK - SUB :]
            return 0

        lax.fori_loop(0, lane_tiles, body, 0)

    def short(index, weight, tile_at):
        held = {
            at: wide[index, tile_at, pl.ds(SUB + at, SUB, stride=run), :]
            for at in range(1 - tap_count, run)
        }
        scale = [taps[weight, pl.ds(i, 1), lanes_of(tile_at)] for i in range(tap_count)]
        for at in range(run):
            total = scale[0] * held[at]
            for i in range(1, tap_count):
                total = total + scale[i] * held[at - i]
            yield at, total

    def gate(owner, group_at):
        tile_at = owner * tiles + group_at
        for (at, first), (_, second) in zip(short(0, 1, tile_at), short(1, 2, tile_at)):
            turned[pl.ds(at, SUB, stride=run), :] = first * second
        gated[owner, group_at] = turned[...].astype(gated.dtype)

    for index in range(3):
        loads[index].wait()
    widen(0)
    widen(1)
    ready(0)
    widen_halo(0)
    ready(1)
    widen_halo(1)

    gated_copies = [[] for _ in range(tiles)]

    def send_gated(d, group_at):
        gated_copies[group_at].append(
            exchange(
                gated.at[peer(d), group_at],
                gated_all.at[group_at],
                gated_send.at[group_at],
                gated_recv.at[group_at],
                d,
            )
        )

    for group_at in range(tiles):
        for d in (*range(1, parts), 0):
            owner = peer(d)
            gate(owner, group_at)
            if d and group_at == 0:
                send_gated(d, group_at)
        gated_all[group_at, me] = gated[me, group_at]

    loads[3].wait()
    widen(2)
    ready(2)
    widen_halo(2)

    def query_step(tile_at, _):
        for at, total in short(2, 0, tile_at):
            query_conv[tile_at, pl.ds(at, SUB, stride=run), :] = total
        return 0

    lax.fori_loop(0, lane_tiles, query_step, 0)

    loads[4].wait()
    loads[5].wait()
    for copy in filter_copies:
        copy.wait_recv()
    for group_at in range(1, tiles):
        for d in range(1, parts):
            send_gated(d, group_at)
    tile = 256

    def transform(first, held):
        return jnp.dot(
            forward[pl.ds(first, tile), :],
            held[...].reshape(tokens, -1),
            preferred_element_type=jnp.float32,
        )

    for first in range(0, 2 * tokens, tile):
        filter_spectrum[pl.ds(first, tile), :] = transform(first, filter_all)

    result_copies = [[] for _ in range(tiles)]
    for group_at in range(tiles):
        for copy in gated_copies[group_at]:
            copy.wait_recv()
        lanes = pl.ds(group_at * LANES, LANES)
        held = gated_all.at[group_at]
        for first in range(0, tokens, tile):
            real, imag = pl.ds(first, tile), pl.ds(tokens + first, tile)
            a, b = transform(first, held), transform(tokens + first, held)
            c, d = filter_spectrum[real, lanes], filter_spectrum[imag, lanes]
            product[group_at, real, :] = (a * c - b * d).astype(product.dtype)
            product[group_at, imag, :] = (a * d + b * c).astype(product.dtype)
        if group_at == 0:
            loads[7].wait()
        for d in (*range(1, parts), 0):
            owner = peer(d)
            result[group_at, owner] = jnp.dot(
                backward[owner], product[group_at], preferred_element_type=jnp.float32
            ).astype(result.dtype)
            if d:
                result_copies[group_at].append(
                    exchange(
                        result.at[group_at, owner],
                        result_all.at[group_at],
                        result_send.at[group_at],
                        result_recv.at[group_at],
                        d,
                    )
                )

    loads[6].wait()
    partial[...] = jnp.zeros_like(partial)

    def finish(owner, group_at, held):
        tile_at = owner * tiles + group_at
        lanes = lanes_of(tile_at)

        def step_body(step, _):
            at = pl.ds(pl.multiple_of(step * block, block), block)
            long_out = held[group_at, owner, at, :].astype(jnp.float32)
            direct = skip[:, lanes] * gated[owner, group_at, at, :].astype(jnp.float32)
            x = query_conv[tile_at, at, :] * (long_out + direct)
            y = x / (1.0 + jnp.exp(-x))
            mixed[at, lanes] = y
            partial[at, :] = partial[at, :] + y * y
            return 0

        lax.fori_loop(0, rows // block, step_body, 0)

    for group_at in range(tiles):
        finish(me, group_at, result)
        for d in range(1, parts):
            result_copies[group_at][d - 1].wait_recv()
            finish(source(d), group_at, result_all)

    power[...] = jnp.broadcast_to(
        jnp.sum(partial[...].T, axis=0, keepdims=True), power.shape
    )
    power_copies = []
    for distance in range(1, groups):
        copy = pltpu.make_async_remote_copy(
            src_ref=power,
            dst_ref=power_all.at[group],
            send_sem=power_send.at[distance - 1],
            recv_sem=power_recv.at[distance - 1],
            device_id={"chan": lax.rem(group + distance, groups)},
            device_id_type=MESH,
        )
        copy.start()
        power_copies.append(copy)
    power_all[group] = power[...]
    for copy in (*halos, *filter_copies, *sum(gated_copies + result_copies, [])):
        copy.wait_send()
    for copy in power_copies:
        copy.wait()
    power_out[...] = jnp.sum(power_all[...], axis=0)


SLICES = 8


def normalize(channels, mixed, power, gain, out, scaled, scale, store_sem):
    rows, width = mixed.shape
    count = rows // SLICES
    row_scale = lax.rsqrt(power[pl.ds(0, 1), :] / channels + 1e-06)
    scale[...] = jnp.broadcast_to(row_scale, (LANES, rows)).T
    stores = []
    for index in range(SLICES):
        at = pl.ds(index * count, count)
        factor = scale[at, :]
        for start in range(0, width, LANES):
            lanes = pl.ds(start, LANES)
            scaled[at, lanes] = mixed[at, lanes] * factor * gain[:, lanes]
        copy = pltpu.make_async_copy(scaled.at[at, :], out.at[at, :], store_sem.at[index])
        copy.start()
        stores.append(copy)
    for copy in stores:
        copy.wait()


def fused(
    query_stream, key_stream, value_stream, short_filters, long_filter, skip_bias, norm_gain
):
    rows, width = query_stream.shape
    parts = lax.axis_size("seq")
    groups = lax.axis_size("chan")
    tokens = rows * parts
    part = width // parts
    tiles = part // LANES
    forward, backward = tables(tokens, parts)
    dma = pltpu.SemaphoreType.DMA
    bf16, f32 = jnp.bfloat16, jnp.float32
    mixed, power = pl.pallas_call(
        functools.partial(kernel, parts, groups),
        out_shape=(pltpu.VMEM((rows, width), f32), pltpu.VMEM((8, rows), f32)),
        in_specs=[pl.BlockSpec(memory_space=pl.ANY)] * 8,
        out_specs=(
            pl.BlockSpec(memory_space=pltpu.VMEM),
            pl.BlockSpec(memory_space=pltpu.VMEM),
        ),
        scratch_shapes=[
            pltpu.VMEM((3, rows + PACK, width), bf16),
            pltpu.VMEM((3, width // LANES, rows + SUB, LANES), f32),
            pltpu.VMEM((rows, LANES), f32),
            pltpu.VMEM(short_filters.shape, f32),
            pltpu.VMEM((1, width), f32),
            pltpu.VMEM(forward.shape, bf16),
            pltpu.VMEM(backward.shape, bf16),
            pltpu.VMEM((parts, rows, part), bf16),
            pltpu.VMEM((parts, tiles, rows, LANES), bf16),
            pltpu.VMEM((tiles, parts, rows, LANES), bf16),
            pltpu.VMEM((width // LANES, rows, LANES), f32),
            pltpu.VMEM((2 * tokens, part), f32),
            pltpu.VMEM((tiles, 2 * tokens, LANES), bf16),
            pltpu.VMEM((tiles, parts, rows, LANES), bf16),
            pltpu.VMEM((tiles, parts, rows, LANES), bf16),
            pltpu.VMEM((rows, LANES), f32),
            pltpu.VMEM((8, rows), f32),
            pltpu.VMEM((groups, 8, rows), f32),
            dma((8,)),
            dma((3,)),
            dma((3,)),
            dma((parts - 1,)),
            dma((parts - 1,)),
            dma((tiles, parts - 1)),
            dma((tiles, parts - 1)),
            dma((tiles, parts - 1)),
            dma((tiles, parts - 1)),
            dma((groups - 1,)),
            dma((groups - 1,)),
        ],
        compiler_params=pltpu.CompilerParams(
            collective_id=0, has_side_effects=True, vmem_limit_bytes=VMEM_BYTES
        ),
    )(
        query_stream,
        key_stream,
        value_stream,
        short_filters,
        long_filter,
        skip_bias[None, :],
        jnp.asarray(forward),
        jnp.asarray(backward),
    )
    return pl.pallas_call(
        functools.partial(normalize, width * groups),
        out_shape=jax.ShapeDtypeStruct((rows, width), f32),
        in_specs=[pl.BlockSpec(memory_space=pltpu.VMEM)] * 3,
        out_specs=pl.BlockSpec(memory_space=pl.ANY),
        scratch_shapes=[
            pltpu.VMEM((rows, width), f32),
            pltpu.VMEM((rows, LANES), f32),
            dma((SLICES,)),
        ],
        compiler_params=pltpu.CompilerParams(vmem_limit_bytes=16 * 1024 * 1024),
    )(mixed, power, norm_gain[None, :])


def dense_fits(mesh, shape):
    tokens, channels = shape
    part = channels // (mesh.shape["chan"] * mesh.shape["seq"])
    rows = tokens // mesh.shape["seq"]
    return (
        part % LANES == 0
        and rows % 256 == 0
        and mesh.shape["seq"] > 1
        and mesh.shape["chan"] > 1
        and 8 * tokens * tokens <= VMEM_BYTES // 4
    )


def solution(mesh):
    placed = (
        P("seq", "chan"),
        P("seq", "chan"),
        P("seq", "chan"),
        P(None, None, "chan"),
        P("seq", "chan"),
        P("chan"),
        P("chan"),
    )

    def apply(query_stream, *others):
        body = fused if dense_fits(mesh, query_stream.shape) else shards
        return jax.shard_map(
            body, mesh=mesh, in_specs=placed, out_specs=P("seq", "chan"), check_vma=False
        )(query_stream, *others)

    return apply
```
